128 devices in a mesh: dp: 4 (over z_lo, core), cp: 32 (over y, x, z_hi).
Axes of the slice: x: 4, y: 4, z: 4 (z_hi: 2, z_lo: 2; z = z_hi * 2 + z_lo), core: 2. Of those that a mesh axis runs over, the one named last changes fastest.
Arguments:
- queries: bfloat16 [32768, 4096], P(('dp', 'cp')), may hold values from -6 to 6
- key_states: bfloat16 [32768, 512], P(('dp', 'cp')), may hold values from -6 to 6
- value_states: bfloat16 [32768, 512], P(('dp', 'cp')), may hold values from -6 to 6
- grad_out: bfloat16 [32768, 4096], P(('dp', 'cp')), may hold values from -6 to 6
- token_weight: float32 [32768], P(('dp', 'cp')), may hold values from 0.1 to 9
- span_size: int32 [4, 32], P('dp'), may hold values from 1 to 8, as said below
- short_lengths: int32 [4, 32, 8], P('dp'), may hold values from 1 to 128, 256 in all within a row
Outputs:
- attn_out: bfloat16 [32768, 4096], P(('dp', 'cp'))
- dquery: bfloat16 [32768, 4096], P(('dp', 'cp'))
- dkey: bfloat16 [32768, 512], P(('dp', 'cp'))
- dvalue: bfloat16 [32768, 512], P(('dp', 'cp'))
The draws below stay inside these ranges and needn't reach their ends.
Inputs may be any that keep to these rules, and one draw needn't show every extreme that they name: `span_size`: along cp, each aligned block of 8 devices of a window is cut into aligned runs of 1, 2, 4 or 8 devices; every device of a run of S devices holds S. Every block of window 0 is one run of 8; window 1's first block holds devices with 1.
All inputs are finite; a program needn't handle non-finite values.
Results may differ from the reference program's by a relative error of at most 0.03.
Values may be sent and summed in bfloat16 or wider, within the bound.
A program may use at most 128 MiB of HBM per device.

```python
import math
import jax
import jax.numpy as jnp
import numpy as np
from jax import lax

HEADS = 32
KV_HEADS = 4
HEAD_DIM = 128
TOK_DEV = 256
SLOTS = 8
SPAN_MAX = 8
ROWS = 32768
N_DP = 4
N_CP = 32


def draw_queries(key, part):
    key = jax.random.fold_in(key, 1)
    array_shape = (ROWS, HEADS * HEAD_DIM)
    return jnp.clip(1.2 * jax.random.normal(key, array_shape, jnp.float32), -6.0, 6.0).astype(jnp.bfloat16)


def draw_key_states(key, part):
    key = jax.random.fold_in(key, 2)
    array_shape = (ROWS, KV_HEADS * HEAD_DIM)
    return jnp.clip(1.2 * jax.random.normal(key, array_shape, jnp.float32), -6.0, 6.0).astype(jnp.bfloat16)


def draw_token_weight(key, part):
    key = jax.random.fold_in(key, 5)
    device_count = ROWS // TOK_DEV
    device_ids = (jnp.arange(ROWS) // TOK_DEV).astype(jnp.float32)
    ramp_share = device_ids / max(device_count - 1, 1)
    base_values = jnp.exp(jax.random.uniform(key, (ROWS,), jnp.float32, math.log(0.1), 0.0))
    return base_values * (1.0 + 2.0 * ramp_share)


def draw_span_size(key, part):
    key = jax.random.fold_in(key, 7)
    pattern_table = jnp.array(np.array([[8, 8, 8, 8, 8, 8, 8, 8], [4, 4, 4, 4, 1, 1, 1, 1], [1, 1, 2, 2, 4, 4, 4, 4], [2, 2, 2, 2, 4, 4, 4, 4], [4, 4, 4, 4, 2, 2, 1, 1], [2, 2, 1, 1, 2, 2, 2, 2]], dtype=np.int32))
    block_count = N_CP // SPAN_MAX
    picks = jax.random.randint(key, (N_DP, block_count), 0, 6)
    picks = picks.at[0, :].set(0).at[1, 0].set(1)
    return pattern_table[picks].reshape(N_DP, N_CP).astype(jnp.int32)


def level_of(own_key, dims, cuts, smallest, high):
    factor_of, own = 1.0, jax.random.fold_in(own_key, 6)
    for dim, parts in cuts:
        steps = jnp.exp(jax.random.uniform(jax.random.fold_in(own, dim), (parts,), jnp.float32, smallest / len(cuts), high / len(cuts)))
        factor_of = factor_of * jnp.repeat(steps, dims[dim] // parts).reshape([-1 if axis == dim else 1 for axis in range(len(dims))])
    return factor_of


def profile(number_of, total, limit, slope):
    weights = [(1 << 20) // math.isqrt(standing ** slope) + 1 for standing in range(2, number_of + 1)]
    spare, holding = total - limit - (number_of - 1), [1] * (number_of - 1)
    while spare > 0:
        candidates = [i for i in range(number_of - 1) if holding[i] < limit]
        mass, left = sum([weights[i] for i in candidates]), spare
        for i in candidates:
            extra = min(limit - holding[i], max(1, left * weights[i] // mass), spare)
            holding[i] = holding[i] + extra
            spare = spare - extra
    return np.array([limit] + holding)


def ragged_sizes(rng, number_of, total, reach, skew):
    if number_of == 2:
        one = jax.random.randint(rng, (), max(1, total - reach), min(reach, total - 1) + 1)
        return jnp.stack([one, total - one])
    sizes = jnp.asarray(profile(number_of, total, reach, skew), jnp.int32)
    couples = (number_of - 1) // 2
    source_of, taker = sizes[1:1 + 2 * couples:2], sizes[2:2 + 2 * couples:2]
    slack = jnp.minimum(source_of - 1, reach - taker)
    shifted = jax.random.randint(jax.random.fold_in(rng, 1), (couples,), 0, 1 << 20) % (slack + 1)
    sizes = sizes.at[1:1 + 2 * couples:2].set(source_of - shifted).at[2:2 + 2 * couples:2].set(taker + shifted)
    return sizes[jax.random.permutation(jax.random.fold_in(rng, 2), number_of)]


def bell_draw(own_key, dims, width, limit, pieces=(), held_as=jnp.bfloat16):
    drawn = jax.random.normal(own_key, dims, jnp.float32) * width
    if len(pieces) > 0:
        drawn = level_of(own_key, dims, pieces, -0.22, 0.18) * drawn
    return jnp.clip(drawn, min=-limit, max=limit).astype(held_as)


def setup_inputs(seed: int = 0) -> dict:
    splits = jax.random.split(jax.random.key(seed), 8)
    return {
        "queries": draw_queries(jax.random.fold_in(splits[7], 71), 0),
        "key_states": draw_key_states(jax.random.fold_in(splits[7], 71), 0),
        "value_states": bell_draw(splits[2], (ROWS, KV_HEADS * HEAD_DIM), 1.0, 6.0, ((0, 128),)),
        "grad_out": bell_draw(splits[3], (ROWS, HEADS * HEAD_DIM), 1.0, 6.0, ((0, 128),)),
        "token_weight": draw_token_weight(jax.random.fold_in(splits[7], 71), 0),
        "span_size": draw_span_size(jax.random.fold_in(splits[7], 71), 0),
        "short_lengths": jax.vmap(lambda own: ragged_sizes(own, SLOTS, TOK_DEV, TOK_DEV // 2, 2))(jax.random.split(splits[6], N_DP * N_CP)).reshape((N_DP, N_CP, SLOTS)).astype(jnp.int32),
    }


NEG = -1e30


def token_meta(span_row, length_rows, device, row_count, slot_count):
    span_len = lax.dynamic_index_in_dim(span_row, device, 0, keepdims=False)
    doc_lengths = lax.dynamic_index_in_dim(length_rows, device, 0, keepdims=False)
    half_rows = row_count // 2
    member_rank = device % span_len
    row_ids = jnp.arange(row_count, dtype=jnp.int32)
    fold_index = jnp.where(row_ids < half_rows, member_rank, 2 * span_len - 1 - member_rank)
    spread_pos = fold_index * half_rows + row_ids % half_rows
    doc_ends = jnp.cumsum(doc_lengths).astype(jnp.int32)
    slot_ids = jnp.sum((row_ids[:, None] >= doc_ends[None, :]).astype(jnp.int32), axis=1)
    doc_starts = (doc_ends - doc_lengths).astype(jnp.int32)
    one_hot = slot_ids[:, None] == jnp.arange(slot_count, dtype=jnp.int32)[None, :]
    local_pos = row_ids - jnp.sum(jnp.where(one_hot, doc_starts[None, :], 0), axis=1)
    spread = span_len > 1
    position = jnp.where(spread, spread_pos, local_pos).astype(jnp.int32)
    document = jnp.where(spread, (device - member_rank) * slot_count, device * slot_count + slot_ids).astype(jnp.int32)
    return position, document


def head_block(query_h, key_h, value_h, dout_h, visible, softmax_scale):
    query_f = query_h.astype(jnp.float32)
    key_f = key_h.astype(jnp.float32)
    value_f = value_h.astype(jnp.float32)
    dout_f = dout_h.astype(jnp.float32)
    scores = jnp.einsum("igd,jd->gij", query_f, key_f) * softmax_scale
    scores = jnp.where(visible[None], scores, NEG)
    row_max = jnp.max(scores, axis=-1, keepdims=True)
    row_sum = jnp.sum(jnp.exp(scores - row_max), axis=-1, keepdims=True)
    log_total = row_max + jnp.log(row_sum)
    probs = jnp.where(visible[None], jnp.exp(scores - log_total), 0.0)
    probs_low = probs.astype(jnp.bfloat16)
    probs_lowf = probs_low.astype(jnp.float32)
    output = jnp.einsum("gij,jd->igd", probs_lowf, value_f).astype(jnp.bfloat16)
    delta = jnp.sum(dout_f * output.astype(jnp.float32), axis=-1)
    dprobs = jnp.einsum("igd,jd->gij", dout_f, value_f)
    dscore = (probs * (dprobs - delta.T[:, :, None])).astype(jnp.bfloat16)
    dscore_f = dscore.astype(jnp.float32)
    dquery = (jnp.einsum("gij,jd->igd", dscore_f, key_f) * softmax_scale).astype(jnp.bfloat16)
    dkey = (jnp.einsum("gij,igd->jd", dscore_f, query_f) * softmax_scale).astype(jnp.bfloat16)
    dvalue = jnp.einsum("gij,igd->jd", probs_lowf, dout_f).astype(jnp.bfloat16)
    return output, dquery, dkey, dvalue


def reference(queries, key_states, value_states, grad_out, token_weight, span_size, short_lengths):
    groups = HEADS // KV_HEADS
    softmax_scale = HEAD_DIM ** -0.5
    block_rows = SPAN_MAX * TOK_DEV
    block_count = ROWS // block_rows
    mean_weight = jnp.sum(token_weight) / ROWS
    dout = (token_weight[:, None] * grad_out.astype(jnp.float32) / mean_weight).astype(jnp.bfloat16)
    device_ids = jnp.arange(N_CP, dtype=jnp.int32)

    def window_meta(span_row, length_rows):
        return jax.vmap(lambda member: token_meta(span_row, length_rows, member, TOK_DEV, SLOTS))(device_ids)

    positions, documents = jax.vmap(window_meta)(span_size, short_lengths)
    positions = positions.reshape(block_count, block_rows)
    documents = documents.reshape(block_count, block_rows)
    query_blocks = queries.reshape(block_count, block_rows, KV_HEADS, groups, HEAD_DIM)
    dout_blocks = dout.reshape(block_count, block_rows, KV_HEADS, groups, HEAD_DIM)
    key_blocks = key_states.reshape(block_count, block_rows, KV_HEADS, HEAD_DIM)
    value_blocks = value_states.reshape(block_count, block_rows, KV_HEADS, HEAD_DIM)

    def one_item(item):
        block_index = item // KV_HEADS
        head_index = item % KV_HEADS

        def take_head(array):
            whole = lax.dynamic_index_in_dim(array, block_index, 0, keepdims=False)
            return lax.dynamic_index_in_dim(whole, head_index, 1, keepdims=False)

        block_pos = lax.dynamic_index_in_dim(positions, block_index, 0, keepdims=False)
        block_doc = lax.dynamic_index_in_dim(documents, block_index, 0, keepdims=False)
        visible = (block_doc[:, None] == block_doc[None, :]) & (block_pos[None, :] <= block_pos[:, None])
        return head_block(take_head(query_blocks), take_head(key_blocks), take_head(value_blocks),
                          take_head(dout_blocks), visible, softmax_scale)

    items = jnp.arange(block_count * KV_HEADS, dtype=jnp.int32)
    output, dquery, dkey, dvalue = lax.map(one_item, items)

    def wide(array):
        shaped = array.reshape(block_count, KV_HEADS, block_rows, groups, HEAD_DIM)
        return jnp.transpose(shaped, (0, 2, 1, 3, 4)).reshape(ROWS, HEADS * HEAD_DIM)

    def narrow(array):
        shaped = array.reshape(block_count, KV_HEADS, block_rows, HEAD_DIM)
        return jnp.transpose(shaped, (0, 2, 1, 3)).reshape(ROWS, KV_HEADS * HEAD_DIM)

    return wide(output), wide(dquery), narrow(dkey), narrow(dvalue)
```

```python
import functools

import jax
import jax.numpy as jnp
from jax import lax
from jax.experimental import pallas as pl
from jax.experimental.pallas import tpu as pltpu
from jax.sharding import PartitionSpec as P

HEADS = 32
KV_HEADS = 4
HEAD_DIM = 128
SPAN_MAX = 8
HALF = 128
ROWS_DEV = 256
SLOTS = 8
GROUPS = HEADS // KV_HEADS
TILES = GROUPS // 2
PAIR = 256
VISITS = 9
NEG = -1e30
SCALE = HEAD_DIM**-0.5
SCALE_LOG2 = SCALE * 1.4426950408889634
F32 = jnp.float32
BF16 = jnp.bfloat16


def dot(a, b):
    return lax.dot_general(a, b, (((1,), (0,)), ((), ())), preferred_element_type=F32)


def dot_nt(a, b):
    return lax.dot_general(a, b, (((1,), (1,)), ((), ())), preferred_element_type=F32)


def kernel(
    n_dp,
    n_blocks,
    q_ref,
    k_ref,
    v_ref,
    g_ref,
    w_ref,
    span_ref,
    len_ref,
    o_ref,
    dq_ref,
    dk_ref,
    dv_ref,
    kv,
    stage,
    inbox,
    own_acc,
    q_t,
    d_t,
    dout,
    bias,
    s_scr,
    p_scr,
    acc,
    row_max,
    row_sum,
    o_acc,
    dq_acc,
    delta,
    qt_scaled,
    dt_scaled,
    sum_block,
    sum_dp,
    sum_y,
    kv_send,
    kv_recv,
    st_send,
    st_recv,
    w_send,
    w_recv,
):
    dp = lax.axis_index("dp")
    cp = lax.axis_index("cp")
    me = lax.rem(cp, SPAN_MAX)
    block = lax.div(cp, SPAN_MAX)
    base = block * SPAN_MAX
    half_me = lax.div(me, 2)
    odd = lax.rem(me, 2)

    def peer_of(step):
        return lax.rem(me + step, SPAN_MAX)

    def at_member(member):
        return (dp, base + member)

    def at_dp(step):
        return (lax.rem(dp + step, n_dp), cp)

    def at_block(step):
        return (dp, lax.rem(block + step, n_blocks) * SPAN_MAX + me)

    barrier = pltpu.get_barrier_semaphore()
    partners = [at_member(peer_of(step)) for step in range(1, SPAN_MAX)]
    partners += [at_dp(step) for step in range(1, n_dp)]
    partners += [at_block(step) for step in range(1, n_blocks)]
    for partner in partners:
        pl.semaphore_signal(barrier, inc=1, device_id=partner, device_id_type=pl.DeviceIdType.MESH)

    def rows_at(half, member):
        return pl.ds(pl.multiple_of((half * SPAN_MAX + member) * HALF, HALF), HALF)

    for head in range(KV_HEADS):
        lanes = slice(head * HEAD_DIM, (head + 1) * HEAD_DIM)
        for half in range(2):
            rows = slice(half * HALF, (half + 1) * HALF)
            kv[head, rows_at(half, me), 0:HEAD_DIM] = k_ref[rows, lanes]
            kv[head, rows_at(half, me), HEAD_DIM : 2 * HEAD_DIM] = v_ref[rows, lanes]

    weight_part = jnp.sum(w_ref[...], axis=1, keepdims=True)
    sum_block[me] = jnp.broadcast_to(weight_part, (8, 128))

    pl.semaphore_wait(barrier, len(partners))

    def remote(src, dst, send_sem, recv_sem, target):
        return pltpu.make_async_remote_copy(
            src_ref=src,
            dst_ref=dst,
            send_sem=send_sem,
            recv_sem=recv_sem,
            device_id=target,
            device_id_type=pl.DeviceIdType.MESH,
        )

    def weight_copy(buffer, slot, offset, step, target, source_slot):
        return remote(
            buffer.at[slot],
            buffer.at[slot],
            w_send.at[offset + step - 1],
            w_recv.at[offset + source_slot],
            target,
        )

    def send_weights(buffer, slot, count, offset, targets):
        for step in range(1, count):
            weight_copy(buffer, slot, offset, step, targets(step), slot).start()

    def wait_weights(buffer, slot, count, offset, targets):
        for step in range(1, count):
            source = lax.rem(slot + step, count)
            weight_copy(buffer, source, offset, step, targets(step), source).wait_recv()
            weight_copy(buffer, slot, offset, step, targets(step), slot).wait_send()
        total = buffer[0]
        for slot_index in range(1, count):
            total = total + buffer[slot_index]
        return total

    def kv_copy(head, half, source, target):
        return remote(
            kv.at[head, rows_at(half, source)],
            kv.at[head, rows_at(half, source)],
            kv_send.at[head, half, target],
            kv_recv.at[head, half, source],
            at_member(target),
        )

    def upper_needed(source, target):
        return (source > target) | ((lax.rem(target, 2) == 1) & (source == target - 1))

    send_weights(sum_block, me, SPAN_MAX, 0, lambda step: at_member(peer_of(step)))

    def send_kv(head, carry):
        for step in range(1, SPAN_MAX):
            peer = peer_of(step)
            kv_copy(head, 0, me, peer).start()

            @pl.when(upper_needed(me, peer))
            def _():
                kv_copy(head, 1, me, peer).start()

        return carry

    lax.fori_loop(0, KV_HEADS, send_kv, 0)

    span = span_ref[0, cp]
    spread = span > 1
    row_id = lax.broadcasted_iota(jnp.int32, (HALF, HALF), 0)
    col_id = lax.broadcasted_iota(jnp.int32, (HALF, HALF), 1)
    slot_of = {}
    for name, ids in (("q0", row_id), ("q1", row_id + HALF), ("k0", col_id), ("k1", col_id + HALF)):
        slot_count = jnp.zeros((HALF, HALF), jnp.int32)
        end = jnp.int32(0)
        for slot in range(SLOTS):
            end = end + len_ref[0, cp, slot]
            slot_count = slot_count + (ids >= end).astype(jnp.int32)
        slot_of[name] = slot_count
    spread_add = jnp.where(spread, 1, 0)

    def same_document(q_name, k_name):
        equal = (slot_of[q_name] == slot_of[k_name]).astype(jnp.int32) + spread_add
        return jnp.where(equal > 0, 0.0, NEG)

    causal = jnp.where(col_id <= row_id, 0.0, NEG)
    own_lower = jnp.minimum(same_document("q0", "k0"), causal)
    own_upper = jnp.minimum(same_document("q1", "k1"), causal)
    own_cross = same_document("q1", "k0")

    def member_bias(member, keep, own):
        seen = jnp.where((lax.bitwise_xor(member, me) < span) & keep, 0.0, NEG)
        is_me = jnp.where(member == me, 1, 0)
        return jnp.where(is_me + jnp.zeros((HALF, HALF), jnp.int32) > 0, own, seen)

    for visit in range(VISITS):
        for side in range(2):
            lanes = slice(side * HALF, (side + 1) * HALF)
            if visit < 4:
                member = jnp.int32(2 * visit + side)
                bias[visit, :, lanes] = member_bias(member, member >= 0, own_cross)
            else:
                extra = visit - 4
                low = member_bias(jnp.int32(2 * extra + side), 2 * extra + side < me, own_lower)
                high = member_bias(jnp.int32(2 * extra - 2 + side), 2 * extra - 2 + side > me, own_upper)
                is_low = jnp.where(extra <= half_me, 1, 0)
                bias[visit, :, lanes] = jnp.where(
                    is_low + jnp.zeros((HALF, HALF), jnp.int32) > 0, low, high
                )

    def turn_queries(index, carry):
        for head in range(2):
            lanes = pl.ds(pl.multiple_of((index * 2 + head) * HEAD_DIM, HEAD_DIM), HEAD_DIM)
            for half in range(2):
                part = q_ref[half * HALF : (half + 1) * HALF, lanes]
                q_t[index, half, :, head * HALF : (head + 1) * HALF] = part.T
        return carry

    lax.fori_loop(0, HEADS // 2, turn_queries, 0)

    block_sum = wait_weights(sum_block, me, SPAN_MAX, 0, lambda step: at_member(peer_of(step)))
    sum_dp[dp] = block_sum
    send_weights(sum_dp, dp, n_dp, 8, at_dp)
    dp_sum = wait_weights(sum_dp, dp, n_dp, 8, at_dp)
    sum_y[block] = dp_sum
    send_weights(sum_y, block, n_blocks, 16, at_block)
    weight_sum = wait_weights(sum_y, block, n_blocks, 16, at_block)
    rows_total = ROWS_DEV * SPAN_MAX * n_dp * n_blocks
    inverse_mean = rows_total / weight_sum[0:1, :]

    for half in range(2):
        rows = slice(half * HALF, (half + 1) * HALF)
        scaled = jnp.broadcast_to(w_ref[0:1, rows] * inverse_mean, (HALF, HALF)).T

        def weigh(index, carry, rows=rows, half=half, scaled=scaled):
            for head in range(2):
                lanes = pl.ds(pl.multiple_of((index * 2 + head) * HEAD_DIM, HEAD_DIM), HEAD_DIM)
                part = (g_ref[rows, lanes].astype(F32) * scaled).astype(BF16)
                dout[rows, lanes] = part
                d_t[index, half, :, head * HALF : (head + 1) * HALF] = part.T
            return carry

        lax.fori_loop(0, HEADS // 2, weigh, 0)

    def half_of(visit):
        if visit < 4 or visit == 8:
            return 1
        if visit == 4:
            return 0
        return jnp.where(visit - 4 <= half_me, 0, 1)

    def pair_of(visit):
        if visit < 4:
            return visit
        if visit == 4:
            return 0
        if visit == 8:
            return 7
        return jnp.where(visit - 4 <= half_me, visit - 4, visit - 1)

    def tile_step(head, tile):
        index = head * TILES + tile

        def lanes_of(part):
            return pl.ds(pl.multiple_of((index * 2 + part) * HEAD_DIM, HEAD_DIM), HEAD_DIM)

        def tall(ref, half):
            rows = pl.ds(half * HALF, HALF) if isinstance(half, int) else pl.ds(pl.multiple_of(half * HALF, HALF), HALF)
            return jnp.concatenate([ref[rows, lanes_of(0)], ref[rows, lanes_of(1)]], axis=0)

        def pair_rows(visit):
            pair = pair_of(visit)
            if isinstance(pair, int):
                return pl.ds(pair * PAIR, PAIR)
            return pl.ds(pl.multiple_of(pair * PAIR, PAIR), PAIR)

        row_max[...] = jnp.full(row_max.shape, NEG, F32)
        row_sum[...] = jnp.zeros(row_sum.shape, F32)
        o_acc[...] = jnp.zeros(o_acc.shape, F32)
        dq_acc[...] = jnp.zeros(dq_acc.shape, F32)

        for visit in range(VISITS):
            half = half_of(visit)
            keys = kv[head, pair_rows(visit), 0:HEAD_DIM]
            masked = bias[visit]
            scores = dot_nt(tall(q_ref, half), keys) * SCALE_LOG2 + jnp.concatenate([masked, masked], axis=0)
            s_scr[visit] = scores
            row_max[half] = jnp.maximum(
                row_max[half], jnp.maximum(scores[:, :HALF], scores[:, HALF:])
            )
        for half in range(2):
            row_max[half] = jnp.broadcast_to(
                jnp.max(row_max[half], axis=1, keepdims=True), (PAIR, HALF)
            )
        for visit in range(VISITS):
            half = half_of(visit)
            values = kv[head, pair_rows(visit), HEAD_DIM : 2 * HEAD_DIM]
            top = row_max[half]
            probs = jnp.exp2(s_scr[visit] - jnp.concatenate([top, top], axis=1))
            row_sum[half] = row_sum[half] + (probs[:, :HALF] + probs[:, HALF:])
            probs = probs.astype(BF16)
            p_scr[visit] = probs
            o_acc[half] = o_acc[half] + dot(probs, values)
        for half in range(2):
            total = jnp.sum(row_sum[half], axis=1, keepdims=True)
            inverse = jnp.broadcast_to(1.0 / total, (PAIR, HALF))
            row_sum[half] = inverse
            out = (o_acc[half] * inverse).astype(BF16)
            rows = slice(half * HALF, (half + 1) * HALF)
            o_ref[rows, lanes_of(0)] = out[:HALF]
            o_ref[rows, lanes_of(1)] = out[HALF:]
            product = tall(dout, half).astype(F32) * out.astype(F32)
            delta[half] = jnp.broadcast_to(jnp.sum(product, axis=1, keepdims=True), (PAIR, HALF))
            turned = jnp.concatenate([inverse[:HALF].T, inverse[HALF:].T], axis=1)
            qt_scaled[half] = (q_t[index, half].astype(F32) * turned).astype(BF16)
            dt_scaled[half] = (d_t[index, half].astype(F32) * turned).astype(BF16)
        for visit in range(VISITS):
            half = half_of(visit)
            pair = pair_of(visit)
            keys = kv[head, pair_rows(visit), 0:HEAD_DIM]
            values = kv[head, pair_rows(visit), HEAD_DIM : 2 * HEAD_DIM]
            dprobs = dot_nt(tall(dout, half), values)
            shift = delta[half]
            probs = p_scr[visit]
            dscore = probs.astype(F32) * (dprobs - jnp.concatenate([shift, shift], axis=1))
            dscore = dscore.astype(BF16)
            dq_acc[half] = dq_acc[half] + dot(dscore, keys)
            acc[pair, 0:HEAD_DIM] = acc[pair, 0:HEAD_DIM] + dot(qt_scaled[half], dscore)
            acc[pair, HEAD_DIM : 2 * HEAD_DIM] = acc[pair, HEAD_DIM : 2 * HEAD_DIM] + dot(
                dt_scaled[half], probs
            )
        for half in range(2):
            result = (dq_acc[half] * (row_sum[half] * SCALE)).astype(BF16)
            rows = slice(half * HALF, (half + 1) * HALF)
            dq_ref[rows, lanes_of(0)] = result[:HALF]
            dq_ref[rows, lanes_of(1)] = result[HALF:]

    def stage_copy(head, half, source, target):
        return remote(
            stage.at[head, half, target],
            inbox.at[head, half, source],
            st_send.at[head, half, target],
            st_recv.at[head, half, source],
            at_member(target),
        )

    def head_step(head, carry):
        for step in range(1, SPAN_MAX):
            peer = peer_of(step)
            kv_copy(head, 0, peer, peer).wait_recv()

            @pl.when(upper_needed(peer, me))
            def _():
                kv_copy(head, 1, peer, peer).wait_recv()

        acc[...] = jnp.zeros(acc.shape, F32)

        def inner(tile, inner_carry):
            tile_step(head, tile)
            return inner_carry

        lax.fori_loop(0, TILES, inner, 0)
        for half in range(2):
            for member in range(SPAN_MAX):
                lanes = slice((member % 2) * HALF, (member % 2 + 1) * HALF)
                part = acc[half * 4 + member // 2, :, lanes]
                stage[head, half, member] = part.astype(BF16)

                @pl.when(member == me)
                def _():
                    own_acc[head, half] = part

        for step in range(1, SPAN_MAX):
            peer = peer_of(step)
            stage_copy(head, 0, me, peer).start()

            @pl.when(peer > me)
            def _():
                stage_copy(head, 1, me, peer).start()

        return carry

    lax.fori_loop(0, KV_HEADS, head_step, 0)

    def finish(head, carry):
        lanes = pl.ds(pl.multiple_of(head * HEAD_DIM, HEAD_DIM), HEAD_DIM)
        for step in range(1, SPAN_MAX):
            peer = peer_of(step)
            stage_copy(head, 0, peer, peer).wait_recv()
            own_acc[head, 0] = own_acc[head, 0] + inbox[head, 0, peer].astype(F32)

            @pl.when(peer < me)
            def _():
                stage_copy(head, 1, peer, peer).wait_recv()
                own_acc[head, 1] = own_acc[head, 1] + inbox[head, 1, peer].astype(F32)

        for half in range(2):
            rows = slice(half * HALF, (half + 1) * HALF)
            dk_ref[rows, lanes] = (own_acc[head, half, 0:HEAD_DIM] * SCALE).T.astype(BF16)
            dv_ref[rows, lanes] = own_acc[head, half, HEAD_DIM : 2 * HEAD_DIM].T.astype(BF16)
        for step in range(1, SPAN_MAX):
            peer = peer_of(step)
            kv_copy(head, 0, me, peer).wait_send()
            stage_copy(head, 0, me, peer).wait_send()

            @pl.when(upper_needed(me, peer))
            def _():
                kv_copy(head, 1, me, peer).wait_send()

            @pl.when(peer > me)
            def _():
                stage_copy(head, 1, me, peer).wait_send()

        return carry

    lax.fori_loop(0, KV_HEADS, finish, 0)


def on_device(n_dp, n_blocks, queries, key_states, value_states, grad_out, token_weight, span_size, short_lengths):
    vmem = pl.BlockSpec(memory_space=pltpu.VMEM)
    smem = pl.BlockSpec(memory_space=pltpu.SMEM)
    wide = jax.ShapeDtypeStruct((ROWS_DEV, HEADS * HEAD_DIM), BF16)
    narrow = jax.ShapeDtypeStruct((ROWS_DEV, KV_HEADS * HEAD_DIM), BF16)
    tile = (2, PAIR, HALF)
    return pl.pallas_call(
        functools.partial(kernel, n_dp, n_blocks),
        out_shape=(wide, wide, narrow, narrow),
        in_specs=[vmem] * 5 + [smem] * 2,
        out_specs=(vmem,) * 4,
        scratch_shapes=[
            pltpu.VMEM((KV_HEADS, 2 * SPAN_MAX * HALF, 2 * HEAD_DIM), BF16),
            pltpu.VMEM((KV_HEADS, 2, SPAN_MAX, 2 * HEAD_DIM, HALF), BF16),
            pltpu.VMEM((KV_HEADS, 2, SPAN_MAX, 2 * HEAD_DIM, HALF), BF16),
            pltpu.VMEM((KV_HEADS, 2, 2 * HEAD_DIM, HALF), F32),
            pltpu.VMEM((HEADS // 2, 2, HEAD_DIM, PAIR), BF16),
            pltpu.VMEM((HEADS // 2, 2, HEAD_DIM, PAIR), BF16),
            pltpu.VMEM((ROWS_DEV, HEADS * HEAD_DIM), BF16),
            pltpu.VMEM((VISITS, HALF, PAIR), F32),
            pltpu.VMEM((VISITS, PAIR, PAIR), F32),
            pltpu.VMEM((VISITS, PAIR, PAIR), BF16),
            pltpu.VMEM((SPAN_MAX, 2 * HEAD_DIM, PAIR), F32),
            pltpu.VMEM(tile, F32),
            pltpu.VMEM(tile, F32),
            pltpu.VMEM(tile, F32),
            pltpu.VMEM(tile, F32),
            pltpu.VMEM(tile, F32),
            pltpu.VMEM((2, HEAD_DIM, PAIR), BF16),
            pltpu.VMEM((2, HEAD_DIM, PAIR), BF16),
            pltpu.VMEM((SPAN_MAX, 8, 128), F32),
            pltpu.VMEM((n_dp, 8, 128), F32),
            pltpu.VMEM((n_blocks, 8, 128), F32),
            pltpu.SemaphoreType.DMA((KV_HEADS, 2, SPAN_MAX)),
            pltpu.SemaphoreType.DMA((KV_HEADS, 2, SPAN_MAX)),
            pltpu.SemaphoreType.DMA((KV_HEADS, 2, SPAN_MAX)),
            pltpu.SemaphoreType.DMA((KV_HEADS, 2, SPAN_MAX)),
            pltpu.SemaphoreType.DMA((24,)),
            pltpu.SemaphoreType.DMA((24,)),
        ],
        compiler_params=pltpu.CompilerParams(
            collective_id=0, has_side_effects=True, vmem_limit_bytes=56 * 1024 * 1024
        ),
    )(
        queries,
        key_states,
        value_states,
        grad_out,
        token_weight.reshape(1, ROWS_DEV),
        span_size,
        short_lengths,
    )


def solution(mesh):
    rows = P(("dp", "cp"), None)
    n_dp = mesh.shape["dp"]
    n_blocks = mesh.shape["cp"] // SPAN_MAX
    return jax.shard_map(
        functools.partial(on_device, n_dp, n_blocks),
        mesh=mesh,
        in_specs=(rows, rows, rows, rows, P(("dp", "cp")), P("dp", None), P("dp", None, None)),
        out_specs=(rows, rows, rows, rows),
        check_vma=False,
    )
```

```python
import functools

import jax
import jax.numpy as jnp
from jax import lax
from jax.experimental import pallas as pl
from jax.experimental.pallas import tpu as pltpu
from jax.sharding import PartitionSpec as P

HEADS = 32
KV_HEADS = 4
HEAD_DIM = 128
SPAN_MAX = 8
HALF = 128
ROWS_DEV = 256
SLOTS = 8
GROUPS = HEADS // KV_HEADS
TILES = GROUPS // 2
PAIR = 256
VISITS = 9
FORWARD_ORDER = (1, 3, 5, 0, 2, 4, 6, 7, 8)
NEG = -1e30
SCALE = HEAD_DIM**-0.5
SCALE_LOG2 = SCALE * 1.4426950408889634
F32 = jnp.float32
BF16 = jnp.bfloat16


def dot(a, b):
    return lax.dot_general(a, b, (((1,), (0,)), ((), ())), preferred_element_type=F32)


def dot_nt(a, b):
    return lax.dot_general(a, b, (((1,), (1,)), ((), ())), preferred_element_type=F32)


def kernel(
    n_dp,
    n_blocks,
    q_hbm,
    k_ref,
    v_ref,
    g_hbm,
    w_ref,
    span_ref,
    len_ref,
    o_hbm,
    dq_hbm,
    dk_ref,
    dv_ref,
    q_ref,
    g_ref,
    o_ref,
    dq_ref,
    kv,
    first_out,
    first_in,
    second_out,
    second_in,
    last_out,
    last_in,
    cross_out,
    cross_in,
    owed_out,
    owed_in,
    q_t,
    d_t,
    dout,
    bias,
    s_scr,
    p_scr,
    acc,
    row_max,
    o_fold,
    dq_acc,
    delta,
    inverses,
    qt_scaled,
    dt_scaled,
    sum_block,
    sum_dp,
    sum_y,
    inverse_mean,
    in_sem,
    out_sem,
    z_send,
    z_recv,
    near_send,
    near_recv,
    far_send,
    far_recv,
    up_send,
    up_recv,
    turn_send,
    turn_recv,
    first_send,
    first_recv,
    second_send,
    second_recv,
    last_send,
    last_recv,
    cross_send,
    cross_recv,
    owed_send,
    owed_recv,
    w_send,
    w_recv,
):
    dp = lax.axis_index("dp")
    cp = lax.axis_index("cp")
    me = lax.rem(cp, SPAN_MAX)
    block = lax.div(cp, SPAN_MAX)
    base = block * SPAN_MAX
    half_me = lax.div(me, 2)
    odd = lax.rem(me, 2)

    def peer_of(step):
        return lax.rem(me + step, SPAN_MAX)

    def at_member(member):
        return (dp, base + member)

    def at_dp(step):
        return (lax.rem(dp + step, n_dp), cp)

    def at_block(step):
        return (dp, lax.rem(block + step, n_blocks) * SPAN_MAX + me)

    barrier = pltpu.get_barrier_semaphore()
    partners = [at_member(peer_of(step)) for step in range(1, SPAN_MAX)]
    partners += [at_dp(step) for step in range(1, n_dp)]
    partners += [at_block(step) for step in range(1, n_blocks)]
    for partner in partners:
        pl.semaphore_signal(barrier, inc=1, device_id=partner, device_id_type=pl.DeviceIdType.MESH)

    across = lax.rem(half_me + 2, 4)
    left = lax.rem(half_me + 3, 4)
    right = lax.rem(half_me + 1, 4)
    own_rows = pl.ds(pl.multiple_of(odd * HALF, HALF), HALF)
    other_rows = pl.ds(pl.multiple_of((1 - odd) * HALF, HALF), HALF)

    def head_lanes(head):
        width = GROUPS * HEAD_DIM
        return pl.ds(pl.multiple_of(head * width, width), width)

    def load_queries(head):
        return pltpu.make_async_copy(
            q_hbm.at[:, head_lanes(head)], q_ref.at[:, head_lanes(head)], in_sem.at[0, head]
        )

    def load_grads(head):
        return pltpu.make_async_copy(
            g_hbm.at[:, head_lanes(head)], g_ref.at[:, head_lanes(head)], in_sem.at[1, head]
        )

    def save_out(head):
        return pltpu.make_async_copy(
            o_ref.at[:, head_lanes(head)], o_hbm.at[:, head_lanes(head)], out_sem.at[0, head]
        )

    def save_dquery(head):
        return pltpu.make_async_copy(
            dq_ref.at[:, head_lanes(head)], dq_hbm.at[:, head_lanes(head)], out_sem.at[1, head]
        )

    for head in range(KV_HEADS):
        load_queries(head).start()
        load_grads(head).start()

    for head in range(KV_HEADS):
        lanes = slice(head * HEAD_DIM, (head + 1) * HEAD_DIM)
        for half in range(2):
            rows = slice(half * HALF, (half + 1) * HALF)
            kv[head, half_me, half, own_rows, 0:HEAD_DIM] = k_ref[rows, lanes]
            kv[head, half_me, half, own_rows, HEAD_DIM : 2 * HEAD_DIM] = v_ref[rows, lanes]

    weight_part = jnp.sum(w_ref[...], axis=1, keepdims=True)
    sum_block[me] = jnp.broadcast_to(weight_part, (8, 128))

    pl.semaphore_wait(barrier, len(partners))

    def remote(src, dst, send_sem, recv_sem, target):
        return pltpu.make_async_remote_copy(
            src_ref=src,
            dst_ref=dst,
            send_sem=send_sem,
            recv_sem=recv_sem,
            device_id=target,
            device_id_type=pl.DeviceIdType.MESH,
        )

    def weight_copy(buffer, slot, offset, step, target, source_slot):
        return remote(
            buffer.at[slot],
            buffer.at[slot],
            w_send.at[offset + step - 1],
            w_recv.at[offset + source_slot],
            target,
        )

    def send_weights(buffer, slot, count, offset, targets):
        for step in range(1, count):
            weight_copy(buffer, slot, offset, step, targets(step), slot).start()

    def wait_weights(buffer, slot, count, offset, targets):
        for step in range(1, count):
            source = lax.rem(slot + step, count)
            weight_copy(buffer, source, offset, step, targets(step), source).wait_recv()
            weight_copy(buffer, slot, offset, step, targets(step), slot).wait_send()
        total = buffer[0]
        for slot_index in range(1, count):
            total = total + buffer[slot_index]
        return total

    partner_at = at_member(lax.bitwise_xor(me, 1))
    left_at = at_member(left * 2 + odd)
    right_at = at_member(right * 2 + odd)

    def rows_of(item):
        return own_rows if item == 0 else other_rows

    def when(condition, step, *given):
        @pl.when(condition)
        def _():
            step(*given)

    sides = (left_at, right_at)

    def partner_copy(head):
        view = kv.at[head, half_me, 0, own_rows]
        return remote(view, view, z_send.at[head], z_recv.at[head], partner_at)

    def near_copy(head, item, way, pair):
        view = kv.at[head, pair, 0, rows_of(item)]
        return remote(view, view, near_send.at[head, item, way], near_recv.at[head, item, way], sides[way])

    def far_copy(head, item, pair):
        view = kv.at[head, pair, 0, rows_of(item)]
        return remote(view, view, far_send.at[head, item], far_recv.at[head, item], right_at)

    def upper_copy(head, source, target):
        view = kv.at[head, source, 1, own_rows]
        return remote(
            view, view, up_send.at[head, target], up_recv.at[head, source], at_member(target * 2 + odd)
        )

    def turned_copy(head, pair, item):
        view = kv.at[head, pair, 1, rows_of(item)]
        return remote(view, view, turn_send.at[head, pair], turn_recv.at[head, pair], partner_at)

    def gather_0(head):
        partner_copy(head).start()
        near_copy(head, 0, 0, half_me).start()
        near_copy(head, 0, 1, half_me).start()
        for target in (0, 1, 2):
            when(target < half_me, lambda: upper_copy(head, half_me, target).start())
        turned_copy(head, half_me, 0).start()

    def gather_1(head):
        partner_copy(head).wait_recv()
        near_copy(head, 1, 0, half_me).start()
        near_copy(head, 1, 1, half_me).start()

    def gather_2(head):
        near_copy(head, 0, 1, left).wait_recv()
        far_copy(head, 0, left).start()
        near_copy(head, 0, 0, right).wait_recv()

    def gather_3(head):
        def turn_on(pair):
            upper_copy(head, pair, half_me).wait_recv()
            turned_copy(head, pair, 0).start()

        for pair in (1, 2, 3):
            when(pair > half_me, turn_on, pair)
        near_copy(head, 1, 1, left).wait_recv()
        far_copy(head, 1, left).start()
        near_copy(head, 1, 0, right).wait_recv()

    def gather_4(head):
        for pair in range(4):
            when(pair >= half_me, lambda: turned_copy(head, pair, 1).wait_recv())
        far_copy(head, 0, across).wait_recv()
        far_copy(head, 1, across).wait_recv()

    def gather_end(head):
        partner_copy(head).wait_send()
        for item in range(2):
            near_copy(head, item, 0, half_me).wait_send()
            near_copy(head, item, 1, half_me).wait_send()
            far_copy(head, item, left).wait_send()
        for target in (0, 1, 2):
            when(target < half_me, lambda: upper_copy(head, half_me, target).wait_send())
        for pair in range(4):
            when(pair >= half_me, lambda: turned_copy(head, pair, 0).wait_send())

    gather_0(0)
    send_weights(sum_block, me, SPAN_MAX, 0, lambda step: at_member(peer_of(step)))

    span = span_ref[0, cp]
    spread = span > 1
    row_id = lax.broadcasted_iota(jnp.int32, (HALF, HALF), 0)
    col_id = lax.broadcasted_iota(jnp.int32, (HALF, HALF), 1)
    slot_of = {}
    for name, ids in (("q0", row_id), ("q1", row_id + HALF), ("k0", col_id), ("k1", col_id + HALF)):
        slot_count = jnp.zeros((HALF, HALF), jnp.int32)
        end = jnp.int32(0)
        for slot in range(SLOTS):
            end = end + len_ref[0, slot, cp]
            slot_count = slot_count + (ids >= end).astype(jnp.int32)
        slot_of[name] = slot_count
    spread_add = jnp.where(spread, 1, 0)

    def same_document(q_name, k_name):
        equal = (slot_of[q_name] == slot_of[k_name]).astype(jnp.int32) + spread_add
        return jnp.where(equal > 0, 0.0, NEG)

    causal = jnp.where(col_id <= row_id, 0.0, NEG)
    own_lower = jnp.minimum(same_document("q0", "k0"), causal)
    own_upper = jnp.minimum(same_document("q1", "k1"), causal)
    own_cross = same_document("q1", "k0")

    partner_seen = jnp.where(span > 1, 0.0, NEG)
    for side in range(2):
        lanes = slice(side * HALF, (side + 1) * HALF)
        is_me = jnp.where(odd == side, 1, 0) + jnp.zeros((HALF, HALF), jnp.int32) > 0
        after = jnp.where(odd > side, 0.0, NEG)
        before = jnp.where(odd < side, 0.0, NEG)
        bias[0, :, lanes] = jnp.where(is_me, own_cross, partner_seen)
        bias[1, :, lanes] = jnp.where(is_me, own_lower, jnp.minimum(partner_seen, after))
        bias[2, :, lanes] = jnp.where(is_me, own_upper, jnp.minimum(partner_seen, before))
    seen = {}
    for visit, pair_step in ((0, 2), (2, 3), (4, 1)):
        other = lax.rem(half_me + pair_step, 4) * 2
        seen[visit] = seen[visit + 1] = jnp.where(lax.bitwise_xor(other, me) < span, 0.0, NEG)

    gather_1(0)

    for head in range(KV_HEADS):
        load_queries(head).wait()

    def turn_queries(index, carry):
        for head in range(2):
            lanes = pl.ds(pl.multiple_of((index * 2 + head) * HEAD_DIM, HEAD_DIM), HEAD_DIM)
            for half in range(2):
                part = q_ref[half * HALF : (half + 1) * HALF, lanes]
                q_t[index, half, :, head * HALF : (head + 1) * HALF] = part.T
        return carry

    lax.fori_loop(0, HEADS // 2, turn_queries, 0)

    gather_2(0)
    gather_0(1)
    for head in range(KV_HEADS):
        load_grads(head).wait()
    for half in range(2):
        rows = slice(half * HALF, (half + 1) * HALF)
        scaled = jnp.broadcast_to(w_ref[0:1, rows], (HALF, HALF)).T

        def weigh(index, carry, rows=rows, half=half, scaled=scaled):
            for head in range(2):
                lanes = pl.ds(pl.multiple_of((index * 2 + head) * HEAD_DIM, HEAD_DIM), HEAD_DIM)
                part = (g_ref[rows, lanes].astype(F32) * scaled).astype(BF16)
                dout[rows, lanes] = part
                d_t[index, half, :, head * HALF : (head + 1) * HALF] = part.T
            return carry

        lax.fori_loop(0, HEADS // 2, weigh, 0)
    gather_3(0)
    gather_1(1)

    def weights_1():
        sum_dp[dp] = wait_weights(sum_block, me, SPAN_MAX, 0, lambda step: at_member(peer_of(step)))
        send_weights(sum_dp, dp, n_dp, 8, at_dp)

    def weights_2():
        sum_y[block] = wait_weights(sum_dp, dp, n_dp, 8, at_dp)
        send_weights(sum_y, block, n_blocks, 16, at_block)

    def weights_3():
        rows_total = ROWS_DEV * SPAN_MAX * n_dp * n_blocks
        inverse_mean[...] = rows_total / wait_weights(sum_y, block, n_blocks, 16, at_block)

    pairs = (across, across, left, left, right, right, half_me, half_me, half_me)

    def half_of(visit):
        if visit in (1, 3, 5):
            return jnp.where(pairs[visit] < half_me, 0, 1)
        return 0 if visit == 7 else 1

    def key_half(visit):
        if visit in (1, 3, 5):
            return jnp.where(pairs[visit] < half_me, 0, 1)
        return 1 if visit == 8 else 0

    def lanes_of(index, part):
        return pl.ds(pl.multiple_of((index * 2 + part) * HEAD_DIM, HEAD_DIM), HEAD_DIM)

    def rows_at(half):
        if isinstance(half, int):
            return pl.ds(half * HALF, HALF)
        return pl.ds(pl.multiple_of(half * HALF, HALF), HALF)

    def keys_of(head, visit):
        return kv[head, pairs[visit], key_half(visit), :, 0:HEAD_DIM]

    def values_of(head, visit):
        return kv[head, pairs[visit], key_half(visit), :, HEAD_DIM : 2 * HEAD_DIM]

    def fold(op, block):
        return op(block[:, :HALF], block[:, HALF:])

    def wide(block):
        return jnp.concatenate([block, block], axis=1)

    def score_steps(head, tile):
        index = head * TILES + tile
        slot = tile % 2
        tops = {}

        def start():
            row_max[slot] = jnp.full(row_max.shape[1:], NEG, F32)

        def score(visit):
            half = half_of(visit)
            keys = keys_of(head, visit)
            for part in range(2):
                scores = dot_nt(q_ref[rows_at(half), lanes_of(index, part)], keys)
                if visit >= 6:
                    scores = scores + bias[visit - 6]
                s_scr[slot, visit, part] = scores
                folded = fold(jnp.maximum, scores)
                if visit < 6:
                    folded = folded + seen[visit]
                if isinstance(half, int):
                    known = tops.get((half, part))
                    tops[half, part] = folded if known is None else jnp.maximum(known, folded)
                else:
                    row_max[slot, half, part] = jnp.maximum(row_max[slot, half, part], folded)

        def end():
            for half in range(2):
                for part in range(2):
                    top = jnp.maximum(row_max[slot, half, part], tops[half, part])
                    row_max[slot, half, part] = jnp.broadcast_to(
                        jnp.max(top, axis=1, keepdims=True), (HALF, HALF)
                    )

        return start, score, end

    def attend_steps(head, tile):
        index = head * TILES + tile
        slot = tile % 2
        kept = {}
        ones = jnp.ones((PAIR, HALF), BF16)

        def start():
            o_fold[...] = jnp.zeros(o_fold.shape, F32)

        def attend(visit):
            half = half_of(visit)
            values = jnp.concatenate([values_of(head, visit), ones], axis=1)
            for part in range(2):
                top = row_max[slot, half, part]
                if visit < 6:
                    top = top - seen[visit]
                probs = jnp.exp2((s_scr[slot, visit, part] - wide(top)) * SCALE_LOG2).astype(BF16)
                p_scr[visit, tile, part * HALF : (part + 1) * HALF, :] = probs
                if isinstance(half, int):
                    kept.setdefault((half, part), []).append((probs, values))
                else:
                    o_fold[half, part] = o_fold[half, part] + dot(probs, values)

        def end():
            for half in range(2):
                rows = slice(half * HALF, (half + 1) * HALF)
                for part in range(2):
                    probs = jnp.concatenate([pair[0] for pair in kept[half, part]], axis=1)
                    values = jnp.concatenate([pair[1] for pair in kept[half, part]], axis=0)
                    both = dot(probs, values) + o_fold[half, part]
                    inverse = 1.0 / both[:, HEAD_DIM:]
                    place = slice(tile * PAIR + part * HALF, tile * PAIR + (part + 1) * HALF)
                    inverses[half, place, :] = inverse
                    out = (both[:, :HEAD_DIM] * inverse).astype(BF16)
                    o_ref[rows, lanes_of(index, part)] = out
                    product = dout[rows, lanes_of(index, part)].astype(F32) * out.astype(F32)
                    delta[half, place, :] = jnp.broadcast_to(
                        jnp.sum(product, axis=1, keepdims=True), (HALF, HALF)
                    )
                    turned = inverse.T
                    lanes = slice(part * HALF, (part + 1) * HALF)
                    qt_scaled[half, tile, :, lanes] = (q_t[index, half, :, lanes].astype(F32) * turned).astype(BF16)
                    dt_scaled[half, tile, :, lanes] = (d_t[index, half, :, lanes].astype(F32) * turned).astype(BF16)

        return start, attend, end

    def forward_step(head, score_tile, attend_tile):
        running = []
        if score_tile is not None:
            running.append(score_steps(head, score_tile))
        if attend_tile is not None:
            running.append(attend_steps(head, attend_tile))
        for steps in running:
            steps[0]()
        for visit in FORWARD_ORDER:
            for steps in running:
                steps[1](visit)
        for steps in running:
            steps[2]()

    def backward_visits(head, visits):
        steps = [(visit, tile) for visit in visits for tile in range(TILES)]
        dprobs = {}

        def begin(step):
            visit, tile = step
            index = head * TILES + tile
            values = values_of(head, visit)
            rows = rows_at(half_of(visit))
            dprobs[step] = [dot_nt(dout[rows, lanes_of(index, part)], values) for part in range(2)]

        begin(steps[0])
        parity = lax.rem(head, 2)
        for number, step in enumerate(steps):
            if number + 1 < len(steps):
                begin(steps[number + 1])
            visit, tile = step
            half = half_of(visit)
            keys = keys_of(head, visit)
            halves = []
            for part in range(2):
                place = slice(tile * PAIR + part * HALF, tile * PAIR + (part + 1) * HALF)
                probs = p_scr[visit, tile, part * HALF : (part + 1) * HALF, :]
                dscore = probs.astype(F32) * (dprobs[step][part] - wide(delta[half, place, :]))
                dscore = dscore.astype(BF16)
                halves.append(dscore)
                dq_acc[half, place, :] = dq_acc[half, place, :] + dot(dscore, keys)
            dk_part = dot(qt_scaled[half, tile], jnp.concatenate(halves, axis=0))
            dv_part = dot(dt_scaled[half, tile], p_scr[visit, tile])
            dkey = dk_part if tile == 0 else dkey + dk_part
            dvalue = dv_part if tile == 0 else dvalue + dv_part
            if tile == TILES - 1:
                pair, side = pairs[visit], key_half(visit)
                acc[parity, pair, side, 0:HEAD_DIM] = acc[parity, pair, side, 0:HEAD_DIM] + dkey
                acc[parity, pair, side, HEAD_DIM : 2 * HEAD_DIM] = (
                    acc[parity, pair, side, HEAD_DIM : 2 * HEAD_DIM] + dvalue
                )

    def close_head(head):
        for tile in range(TILES):
            index = head * TILES + tile
            tile_rows = slice(tile * PAIR, (tile + 1) * PAIR)
            for half in range(2):
                result = (
                    dq_acc[half, tile_rows, :] * (inverses[half, tile_rows, :] * (inverse_mean[0:1, :] * SCALE))
                ).astype(BF16)
                rows = slice(half * HALF, (half + 1) * HALF)
                dq_ref[rows, lanes_of(index, 0)] = result[:HALF]
                dq_ref[rows, lanes_of(index, 1)] = result[HALF:]

    def first_copy(head):
        return remote(first_out.at[head], first_in.at[head], first_send.at[head], first_recv.at[head], left_at)

    def second_copy(head, way):
        return remote(
            second_out.at[head, way],
            second_in.at[head, way],
            second_send.at[head, way],
            second_recv.at[head, way],
            sides[way],
        )

    def last_copy(head):
        return remote(last_out.at[head], last_in.at[head], last_send.at[head], last_recv.at[head], partner_at)

    def cross_copy(head, pair):
        return remote(
            cross_out.at[head, pair],
            cross_in.at[head, pair],
            cross_send.at[head, pair],
            cross_recv.at[head, pair],
            partner_at,
        )

    def owed_copy(head, source, target):
        return remote(
            owed_out.at[head, target],
            owed_in.at[head, source],
            owed_send.at[head, target],
            owed_recv.at[head, source],
            at_member(target * 2 + odd),
        )

    def cross_start(head, pair):
        cross_out[head, pair] = acc[lax.rem(head, 2), pair, 1, :, other_rows].astype(BF16)
        cross_copy(head, pair).start()

    def scatter_1(head):
        first_out[head] = acc[lax.rem(head, 2), across, 0].astype(BF16)
        first_copy(head).start()
        when(half_me < 2, cross_start, head, across)

    def scatter_2(head):
        second_out[head, 1] = acc[lax.rem(head, 2), right, 0].astype(BF16)
        second_copy(head, 1).start()
        when(half_me < 3, cross_start, head, right)
        when(half_me == 0, cross_start, head, left)

    def scatter_3(head):
        cross_start(head, half_me)
        first_copy(head).wait_recv()
        second_out[head, 0] = (acc[lax.rem(head, 2), left, 0] + first_in[head].astype(F32)).astype(BF16)
        second_copy(head, 0).start()

    def scatter_4(head):
        def pay(pair):
            cross_copy(head, pair).wait_recv()
            total = acc[lax.rem(head, 2), pair, 1, :, own_rows] + cross_in[head, pair].astype(F32)
            owed_out[head, pair] = total.astype(BF16)
            owed_copy(head, half_me, pair).start()

        for pair in (1, 2, 3):
            when(pair > half_me, pay, pair)

    def scatter_5(head):
        parity = lax.rem(head, 2)
        second_copy(head, 0).wait_recv()
        second_copy(head, 1).wait_recv()
        acc[parity, half_me, 0] = acc[parity, half_me, 0] + (
            second_in[head, 0].astype(F32) + second_in[head, 1].astype(F32)
        )
        last_out[head] = acc[parity, half_me, 0, :, other_rows].astype(BF16)
        last_copy(head).start()

    def scatter_6(head):
        parity = lax.rem(head, 2)
        lanes = pl.ds(pl.multiple_of(head * HEAD_DIM, HEAD_DIM), HEAD_DIM)

        def settle(side, total):
            rows = slice(side * HALF, (side + 1) * HALF)
            scale = inverse_mean[0:1, :]
            dk_ref[rows, lanes] = (total[:HEAD_DIM] * (scale * SCALE)).T.astype(BF16)
            dv_ref[rows, lanes] = (total[HEAD_DIM:] * scale).T.astype(BF16)

        def collect(source):
            owed_copy(head, source, half_me).wait_recv()
            acc[parity, half_me, 1, :, own_rows] = acc[parity, half_me, 1, :, own_rows] + owed_in[
                head, source
            ].astype(F32)

        for source in (0, 1, 2):
            when(source < half_me, collect, source)
        cross_copy(head, half_me).wait_recv()
        settle(1, acc[parity, half_me, 1, :, own_rows] + cross_in[head, half_me].astype(F32))
        last_copy(head).wait_recv()
        settle(0, acc[parity, half_me, 0, :, own_rows] + last_in[head].astype(F32))

    def scatter_end(head):
        first_copy(head).wait_send()
        second_copy(head, 0).wait_send()
        second_copy(head, 1).wait_send()
        last_copy(head).wait_send()
        for pair in range(4):
            when(pair >= half_me, lambda: cross_copy(head, pair).wait_send())
        for pair in (1, 2, 3):
            when(pair > half_me, lambda: owed_copy(head, half_me, pair).wait_send())

    def head_step(head, carry):
        gather_4(head)
        acc[lax.rem(head, 2)] = jnp.zeros(acc.shape[1:], F32)
        dq_acc[...] = jnp.zeros(dq_acc.shape, F32)
        more = head < KV_HEADS - 1
        earlier = head > 0

        first = head == 0

        forward_step(head, 0, None)
        when(more, gather_2, head + 1)
        when(first, weights_1)
        forward_step(head, 1, 0)
        when(first, weights_2)
        when(earlier, scatter_4, head - 1)
        forward_step(head, 2, 1)
        when(more, gather_3, head + 1)
        when(first, weights_3)
        forward_step(head, 3, 2)
        forward_step(head, None, 3)
        save_out(head).start()
        when(head < KV_HEADS - 2, gather_0, head + 2)
        backward_visits(head, (0, 1))
        scatter_1(head)
        when(earlier, scatter_5, head - 1)
        backward_visits(head, (2, 3, 4, 5))
        scatter_2(head)
        when(head < KV_HEADS - 2, gather_1, head + 2)
        backward_visits(head, (6, 7, 8))
        scatter_3(head)
        close_head(head)
        save_dquery(head).start()
        when(earlier, scatter_6, head - 1)
        return carry

    lax.fori_loop(0, KV_HEADS, head_step, 0)
    scatter_4(KV_HEADS - 1)
    scatter_5(KV_HEADS - 1)
    scatter_6(KV_HEADS - 1)

    def finish(head, carry):
        gather_end(head)
        scatter_end(head)
        save_out(head).wait()
        save_dquery(head).wait()
        return carry

    lax.fori_loop(0, KV_HEADS, finish, 0)


CHUNKS = 4


def carry_kernel(count, *refs):
    sources, targets, slots = refs[:count], refs[count : 2 * count], refs[2 * count : 3 * count]
    sem = refs[3 * count]

    def copies(number, chunk):
        rows = sources[number].shape[0] // CHUNKS
        place = pl.ds(chunk * rows, rows)
        arrive = pltpu.make_async_copy(
            sources[number].at[place], slots[number].at[place], sem.at[0, number, chunk]
        )
        leave = pltpu.make_async_copy(
            slots[number].at[place], targets[number].at[place], sem.at[1, number, chunk]
        )
        return arrive, leave

    steps = [copies(number, chunk) for chunk in range(CHUNKS) for number in range(count)]
    for arrive, _ in steps:
        arrive.start()
    for arrive, leave in steps:
        arrive.wait()
        leave.start()
    for _, leave in steps:
        leave.wait()


def carry_out(*arrays):
    hbm = pl.BlockSpec(memory_space=pl.ANY)
    count = len(arrays)
    return pl.pallas_call(
        functools.partial(carry_kernel, count),
        out_shape=tuple(jax.ShapeDtypeStruct(array.shape, array.dtype) for array in arrays),
        in_specs=[hbm] * count,
        out_specs=(hbm,) * count,
        scratch_shapes=[pltpu.VMEM(array.shape, array.dtype) for array in arrays]
        + [pltpu.SemaphoreType.DMA((2, count, CHUNKS))],
        compiler_params=pltpu.CompilerParams(vmem_limit_bytes=56 * 1024 * 1024),
    )(*arrays)


def on_device(n_dp, n_blocks, queries, key_states, value_states, grad_out, token_weight, span_size, short_lengths):
    vmem = pl.BlockSpec(memory_space=pltpu.VMEM)
    smem = pl.BlockSpec(memory_space=pltpu.SMEM)
    hbm = pl.BlockSpec(memory_space=pl.ANY)
    wide = jax.ShapeDtypeStruct((ROWS_DEV, HEADS * HEAD_DIM), BF16)
    narrow = jax.ShapeDtypeStruct((ROWS_DEV, KV_HEADS * HEAD_DIM), BF16)
    all_rows = (2, TILES * PAIR, HEAD_DIM)
    results = pl.pallas_call(
        functools.partial(kernel, n_dp, n_blocks),
        out_shape=(wide, wide, narrow, narrow),
        in_specs=[hbm, vmem, vmem, hbm, vmem, smem, smem],
        out_specs=(hbm, hbm, vmem, vmem),
        scratch_shapes=[
            pltpu.VMEM((ROWS_DEV, HEADS * HEAD_DIM), BF16),
            pltpu.VMEM((ROWS_DEV, HEADS * HEAD_DIM), BF16),
            pltpu.VMEM((ROWS_DEV, HEADS * HEAD_DIM), BF16),
            pltpu.VMEM((ROWS_DEV, HEADS * HEAD_DIM), BF16),
            pltpu.VMEM((KV_HEADS, 4, 2, PAIR, 2 * HEAD_DIM), BF16),
            pltpu.VMEM((KV_HEADS, 2 * HEAD_DIM, PAIR), BF16),
            pltpu.VMEM((KV_HEADS, 2 * HEAD_DIM, PAIR), BF16),
            pltpu.VMEM((KV_HEADS, 2, 2 * HEAD_DIM, PAIR), BF16),
            pltpu.VMEM((KV_HEADS, 2, 2 * HEAD_DIM, PAIR), BF16),
            pltpu.VMEM((KV_HEADS, 2 * HEAD_DIM, HALF), BF16),
            pltpu.VMEM((KV_HEADS, 2 * HEAD_DIM, HALF), BF16),
            pltpu.VMEM((KV_HEADS, 4, 2 * HEAD_DIM, HALF), BF16),
            pltpu.VMEM((KV_HEADS, 4, 2 * HEAD_DIM, HALF), BF16),
            pltpu.VMEM((KV_HEADS, 4, 2 * HEAD_DIM, HALF), BF16),
            pltpu.VMEM((KV_HEADS, 4, 2 * HEAD_DIM, HALF), BF16),
            pltpu.VMEM((HEADS // 2, 2, HEAD_DIM, PAIR), BF16),
            pltpu.VMEM((HEADS // 2, 2, HEAD_DIM, PAIR), BF16),
            pltpu.VMEM((ROWS_DEV, HEADS * HEAD_DIM), BF16),
            pltpu.VMEM((3, HALF, PAIR), F32),
            pltpu.VMEM((2, VISITS, 2, HALF, PAIR), F32),
            pltpu.VMEM((VISITS, TILES, PAIR, PAIR), BF16),
            pltpu.VMEM((2, 4, 2, 2 * HEAD_DIM, PAIR), F32),
            pltpu.VMEM((2, 2, 2, HALF, HALF), F32),
            pltpu.VMEM((2, 2, HALF, PAIR), F32),
            pltpu.VMEM(all_rows, F32),
            pltpu.VMEM(all_rows, F32),
            pltpu.VMEM(all_rows, F32),
            pltpu.VMEM((2, TILES, HEAD_DIM, PAIR), BF16),
            pltpu.VMEM((2, TILES, HEAD_DIM, PAIR), BF16),
            pltpu.VMEM((SPAN_MAX, 8, 128), F32),
            pltpu.VMEM((n_dp, 8, 128), F32),
            pltpu.VMEM((n_blocks, 8, 128), F32),
            pltpu.VMEM((8, 128), F32),
            pltpu.SemaphoreType.DMA((2, KV_HEADS)),
            pltpu.SemaphoreType.DMA((2, KV_HEADS)),
            pltpu.SemaphoreType.DMA((KV_HEADS,)),
            pltpu.SemaphoreType.DMA((KV_HEADS,)),
            pltpu.SemaphoreType.DMA((KV_HEADS, 2, 2)),
            pltpu.SemaphoreType.DMA((KV_HEADS, 2, 2)),
            pltpu.SemaphoreType.DMA((KV_HEADS, 2)),
            pltpu.SemaphoreType.DMA((KV_HEADS, 2)),
            pltpu.SemaphoreType.DMA((KV_HEADS, 4)),
            pltpu.SemaphoreType.DMA((KV_HEADS, 4)),
            pltpu.SemaphoreType.DMA((KV_HEADS, 4)),
            pltpu.SemaphoreType.DMA((KV_HEADS, 4)),
            pltpu.SemaphoreType.DMA((KV_HEADS,)),
            pltpu.SemaphoreType.DMA((KV_HEADS,)),
            pltpu.SemaphoreType.DMA((KV_HEADS, 2)),
            pltpu.SemaphoreType.DMA((KV_HEADS, 2)),
            pltpu.SemaphoreType.DMA((KV_HEADS,)),
            pltpu.SemaphoreType.DMA((KV_HEADS,)),
            pltpu.SemaphoreType.DMA((KV_HEADS, 4)),
            pltpu.SemaphoreType.DMA((KV_HEADS, 4)),
            pltpu.SemaphoreType.DMA((KV_HEADS, 4)),
            pltpu.SemaphoreType.DMA((KV_HEADS, 4)),
            pltpu.SemaphoreType.DMA((24,)),
            pltpu.SemaphoreType.DMA((24,)),
        ],
        compiler_params=pltpu.CompilerParams(
            collective_id=0, has_side_effects=True, vmem_limit_bytes=56 * 1024 * 1024
        ),
    )(
        queries,
        key_states,
        value_states,
        grad_out,
        token_weight.reshape(1, ROWS_DEV),
        span_size,
        jnp.swapaxes(short_lengths, 1, 2),
    )
    return carry_out(*results)


def solution(mesh):
    rows = P(("dp", "cp"), None)
    n_dp = mesh.shape["dp"]
    n_blocks = mesh.shape["cp"] // SPAN_MAX
    return jax.shard_map(
        functools.partial(on_device, n_dp, n_blocks),
        mesh=mesh,
        in_specs=(rows, rows, rows, rows, P(("dp", "cp")), P("dp", None), P("dp", None, None)),
        out_specs=(rows, rows, rows, rows),
        check_vma=False,
    )
```

```python
import functools

import jax
import jax.numpy as jnp
from jax import lax
from jax.experimental import pallas as pl
from jax.experimental.pallas import tpu as pltpu
from jax.sharding import PartitionSpec as P

HEADS = 32
KV_HEADS = 4
HEAD_DIM = 128
SPAN_MAX = 8
HALF = 128
ROWS_DEV = 256
SLOTS = 8
GROUPS = HEADS // KV_HEADS
TILES = GROUPS // 2
PAIR = 256
VISITS = 9
FORWARD_ORDER = (1, 3, 5, 0, 2, 4, 6, 7, 8)
NEG = -1e30
SCALE = HEAD_DIM**-0.5
SCALE_LOG2 = SCALE * 1.4426950408889634
F32 = jnp.float32
BF16 = jnp.bfloat16


def dot(a, b):
    return lax.dot_general(a, b, (((1,), (0,)), ((), ())), preferred_element_type=F32)


def dot_nt(a, b):
    return lax.dot_general(a, b, (((1,), (1,)), ((), ())), preferred_element_type=F32)


def kernel(
    n_dp,
    n_blocks,
    q_hbm,
    k_ref,
    v_ref,
    g_hbm,
    w_ref,
    span_ref,
    len_ref,
    o_hbm,
    dq_hbm,
    dk_ref,
    dv_ref,
    q_ref,
    g_ref,
    o_ref,
    dq_ref,
    kv,
    first_out,
    first_in,
    second_out,
    second_in,
    last_out,
    last_in,
    cross_out,
    cross_in,
    owed_out,
    owed_in,
    q_t,
    d_t,
    dout,
    bias,
    s_scr,
    p_scr,
    acc,
    row_max,
    o_fold,
    dq_acc,
    delta,
    inverses,
    qt_scaled,
    dt_scaled,
    sum_block,
    sum_dp,
    sum_y,
    inverse_mean,
    in_sem,
    out_sem,
    z_send,
    z_recv,
    near_send,
    near_recv,
    far_send,
    far_recv,
    up_send,
    up_recv,
    turn_send,
    turn_recv,
    first_send,
    first_recv,
    second_send,
    second_recv,
    last_send,
    last_recv,
    cross_send,
    cross_recv,
    owed_send,
    owed_recv,
    w_send,
    w_recv,
):
    dp = lax.axis_index("dp")
    cp = lax.axis_index("cp")
    me = lax.rem(cp, SPAN_MAX)
    block = lax.div(cp, SPAN_MAX)
    base = block * SPAN_MAX
    half_me = lax.div(me, 2)
    odd = lax.rem(me, 2)

    def peer_of(step):
        return lax.rem(me + step, SPAN_MAX)

    def at_member(member):
        return (dp, base + member)

    def at_dp(step):
        return (lax.rem(dp + step, n_dp), cp)

    def at_block(step):
        return (dp, lax.rem(block + step, n_blocks) * SPAN_MAX + me)

    barrier = pltpu.get_barrier_semaphore()
    partners = [at_member(peer_of(step)) for step in range(1, SPAN_MAX)]
    partners += [at_dp(step) for step in range(1, n_dp)]
    partners += [at_block(step) for step in range(1, n_blocks)]
    for partner in partners:
        pl.semaphore_signal(barrier, inc=1, device_id=partner, device_id_type=pl.DeviceIdType.MESH)

    across = lax.rem(half_me + 2, 4)
    left = lax.rem(half_me + 3, 4)
    right = lax.rem(half_me + 1, 4)
    own_rows = pl.ds(pl.multiple_of(odd * HALF, HALF), HALF)
    other_rows = pl.ds(pl.multiple_of((1 - odd) * HALF, HALF), HALF)

    def head_lanes(head):
        width = GROUPS * HEAD_DIM
        return pl.ds(pl.multiple_of(head * width, width), width)

    def load_queries(head):
        return pltpu.make_async_copy(
            q_hbm.at[:, head_lanes(head)], q_ref.at[:, head_lanes(head)], in_sem.at[0, head]
        )

    def load_grads(head):
        return pltpu.make_async_copy(
            g_hbm.at[:, head_lanes(head)], g_ref.at[:, head_lanes(head)], in_sem.at[1, head]
        )

    def save_out(head):
        return pltpu.make_async_copy(
            o_ref.at[:, head_lanes(head)], o_hbm.at[:, head_lanes(head)], out_sem.at[0, head]
        )

    def save_dquery(head):
        return pltpu.make_async_copy(
            dq_ref.at[:, head_lanes(head)], dq_hbm.at[:, head_lanes(head)], out_sem.at[1, head]
        )

    for head in range(KV_HEADS):
        load_queries(head).start()
        load_grads(head).start()

    for head in range(KV_HEADS):
        lanes = slice(head * HEAD_DIM, (head + 1) * HEAD_DIM)
        for half in range(2):
            rows = slice(half * HALF, (half + 1) * HALF)
            kv[head, half_me, half, own_rows, 0:HEAD_DIM] = k_ref[rows, lanes]
            kv[head, half_me, half, own_rows, HEAD_DIM : 2 * HEAD_DIM] = v_ref[rows, lanes]

    weight_part = jnp.sum(w_ref[...], axis=1, keepdims=True)
    sum_block[me] = jnp.broadcast_to(weight_part, (8, 128))

    pl.semaphore_wait(barrier, len(partners))

    def remote(src, dst, send_sem, recv_sem, target):
        return pltpu.make_async_remote_copy(
            src_ref=src,
            dst_ref=dst,
            send_sem=send_sem,
            recv_sem=recv_sem,
            device_id=target,
            device_id_type=pl.DeviceIdType.MESH,
        )

    def weight_copy(buffer, slot, offset, step, target, source_slot):
        return remote(
            buffer.at[slot],
            buffer.at[slot],
            w_send.at[offset + step - 1],
            w_recv.at[offset + source_slot],
            target,
        )

    def send_weights(buffer, slot, count, offset, targets):
        for step in range(1, count):
            weight_copy(buffer, slot, offset, step, targets(step), slot).start()

    def wait_weights(buffer, slot, count, offset, targets):
        for step in range(1, count):
            source = lax.rem(slot + step, count)
            weight_copy(buffer, source, offset, step, targets(step), source).wait_recv()
            weight_copy(buffer, slot, offset, step, targets(step), slot).wait_send()
        total = buffer[0]
        for slot_index in range(1, count):
            total = total + buffer[slot_index]
        return total

    partner_at = at_member(lax.bitwise_xor(me, 1))
    left_at = at_member(left * 2 + odd)
    right_at = at_member(right * 2 + odd)

    def rows_of(item):
        return own_rows if item == 0 else other_rows

    def when(condition, step, *given):
        @pl.when(condition)
        def _():
            step(*given)

    sides = (left_at, right_at)

    def partner_copy(head):
        view = kv.at[head, half_me, 0, own_rows]
        return remote(view, view, z_send.at[head], z_recv.at[head], partner_at)

    def near_copy(head, item, way, pair):
        view = kv.at[head, pair, 0, rows_of(item)]
        return remote(view, view, near_send.at[head, item, way], near_recv.at[head, item, way], sides[way])

    def far_copy(head, item, pair):
        view = kv.at[head, pair, 0, rows_of(item)]
        return remote(view, view, far_send.at[head, item], far_recv.at[head, item], sides[1 - item])

    def upper_copy(head, source, target):
        view = kv.at[head, source, 1, own_rows]
        return remote(
            view, view, up_send.at[head, target], up_recv.at[head, source], at_member(target * 2 + odd)
        )

    def turned_copy(head, pair, item):
        view = kv.at[head, pair, 1, rows_of(item)]
        return remote(view, view, turn_send.at[head, pair], turn_recv.at[head, pair], partner_at)

    def gather_0(head):
        partner_copy(head).start()
        near_copy(head, 0, 0, half_me).start()
        near_copy(head, 0, 1, half_me).start()
        for target in (0, 1, 2):
            when(target < half_me, lambda: upper_copy(head, half_me, target).start())
        turned_copy(head, half_me, 0).start()

    def gather_1(head):
        partner_copy(head).wait_recv()
        near_copy(head, 1, 0, half_me).start()
        near_copy(head, 1, 1, half_me).start()

    def gather_2(head):
        near_copy(head, 0, 1, left).wait_recv()
        far_copy(head, 0, left).start()
        near_copy(head, 0, 0, right).wait_recv()

    def gather_turn(head):
        def turn_on(pair):
            upper_copy(head, pair, half_me).wait_recv()
            turned_copy(head, pair, 0).start()

        for pair in (1, 2, 3):
            when(pair > half_me, turn_on, pair)

    def gather_forward(head):
        near_copy(head, 1, 0, right).wait_recv()
        far_copy(head, 1, right).start()
        near_copy(head, 1, 1, left).wait_recv()

    def gather_3(head):
        gather_turn(head)
        gather_forward(head)

    def gather_4(head):
        for pair in range(4):
            when(pair >= half_me, lambda: turned_copy(head, pair, 1).wait_recv())
        far_copy(head, 0, across).wait_recv()
        far_copy(head, 1, across).wait_recv()

    def gather_end(head):
        partner_copy(head).wait_send()
        for item in range(2):
            near_copy(head, item, 0, half_me).wait_send()
            near_copy(head, item, 1, half_me).wait_send()
            far_copy(head, item, (left, right)[item]).wait_send()
        for target in (0, 1, 2):
            when(target < half_me, lambda: upper_copy(head, half_me, target).wait_send())
        for pair in range(4):
            when(pair >= half_me, lambda: turned_copy(head, pair, 0).wait_send())

    gather_0(0)
    send_weights(sum_block, me, SPAN_MAX, 0, lambda step: at_member(peer_of(step)))

    span = span_ref[0, cp]
    spread = span > 1
    row_id = lax.broadcasted_iota(jnp.int32, (HALF, HALF), 0)
    col_id = lax.broadcasted_iota(jnp.int32, (HALF, HALF), 1)
    slot_of = {}
    for name, ids in (("q0", row_id), ("q1", row_id + HALF), ("k0", col_id), ("k1", col_id + HALF)):
        slot_count = jnp.zeros((HALF, HALF), jnp.int32)
        end = jnp.int32(0)
        for slot in range(SLOTS):
            end = end + len_ref[0, slot, cp]
            slot_count = slot_count + (ids >= end).astype(jnp.int32)
        slot_of[name] = slot_count
    spread_add = jnp.where(spread, 1, 0)

    def same_document(q_name, k_name):
        equal = (slot_of[q_name] == slot_of[k_name]).astype(jnp.int32) + spread_add
        return jnp.where(equal > 0, 0.0, NEG)

    causal = jnp.where(col_id <= row_id, 0.0, NEG)
    own_lower = jnp.minimum(same_document("q0", "k0"), causal)
    own_upper = jnp.minimum(same_document("q1", "k1"), causal)
    own_cross = same_document("q1", "k0")

    partner_seen = jnp.where(span > 1, 0.0, NEG)
    for side in range(2):
        lanes = slice(side * HALF, (side + 1) * HALF)
        is_me = jnp.where(odd == side, 1, 0) + jnp.zeros((HALF, HALF), jnp.int32) > 0
        after = jnp.where(odd > side, 0.0, NEG)
        before = jnp.where(odd < side, 0.0, NEG)
        bias[0, :, lanes] = jnp.where(is_me, own_cross, partner_seen)
        bias[1, :, lanes] = jnp.where(is_me, own_lower, jnp.minimum(partner_seen, after))
        bias[2, :, lanes] = jnp.where(is_me, own_upper, jnp.minimum(partner_seen, before))
    seen = {}
    for visit, pair_step in ((0, 2), (2, 3), (4, 1)):
        other = lax.rem(half_me + pair_step, 4) * 2
        seen[visit] = seen[visit + 1] = jnp.where(lax.bitwise_xor(other, me) < span, 0.0, NEG)

    gather_1(0)
    gather_turn(0)
    gather_2(0)
    gather_0(1)
    gather_forward(0)

    def prepare(head):
        load_queries(head).wait()
        load_grads(head).wait()
        scaled = [jnp.broadcast_to(w_ref[0:1, half * HALF : (half + 1) * HALF], (HALF, HALF)).T for half in range(2)]

        def turn(tile, carry):
            index = head * TILES + tile
            for part in range(2):
                lanes = pl.ds(pl.multiple_of((index * 2 + part) * HEAD_DIM, HEAD_DIM), HEAD_DIM)
                columns = slice(part * HALF, (part + 1) * HALF)
                for half in range(2):
                    rows = slice(half * HALF, (half + 1) * HALF)
                    q_t[index, half, :, columns] = q_ref[rows, lanes].T
                    weighted = (g_ref[rows, lanes].astype(F32) * scaled[half]).astype(BF16)
                    dout[rows, lanes] = weighted
                    d_t[index, half, :, columns] = weighted.T
            return carry

        lax.fori_loop(0, TILES, turn, 0)

    prepare(0)

    def weights_1():
        sum_dp[dp] = wait_weights(sum_block, me, SPAN_MAX, 0, lambda step: at_member(peer_of(step)))
        send_weights(sum_dp, dp, n_dp, 8, at_dp)

    def weights_2():
        sum_y[block] = wait_weights(sum_dp, dp, n_dp, 8, at_dp)
        send_weights(sum_y, block, n_blocks, 16, at_block)

    def weights_3():
        rows_total = ROWS_DEV * SPAN_MAX * n_dp * n_blocks
        inverse_mean[...] = rows_total / wait_weights(sum_y, block, n_blocks, 16, at_block)

    pairs = (across, across, left, left, right, right, half_me, half_me, half_me)

    def half_of(visit):
        if visit in (1, 3, 5):
            return jnp.where(pairs[visit] < half_me, 0, 1)
        return 0 if visit == 7 else 1

    def key_half(visit):
        if visit in (1, 3, 5):
            return jnp.where(pairs[visit] < half_me, 0, 1)
        return 1 if visit == 8 else 0

    def lanes_of(index, part):
        return pl.ds(pl.multiple_of((index * 2 + part) * HEAD_DIM, HEAD_DIM), HEAD_DIM)

    def rows_at(half):
        if isinstance(half, int):
            return pl.ds(half * HALF, HALF)
        return pl.ds(pl.multiple_of(half * HALF, HALF), HALF)

    def keys_of(head, visit):
        return kv[head, pairs[visit], key_half(visit), :, 0:HEAD_DIM]

    def values_of(head, visit):
        return kv[head, pairs[visit], key_half(visit), :, HEAD_DIM : 2 * HEAD_DIM]

    def fold(op, block):
        return op(block[:, :HALF], block[:, HALF:])

    def wide(block):
        return jnp.concatenate([block, block], axis=1)

    def score_steps(head, tile):
        index = head * TILES + tile
        slot = tile % 2
        tops = {}

        def start():
            row_max[slot] = jnp.full(row_max.shape[1:], NEG, F32)

        def score(visit):
            half = half_of(visit)
            keys = keys_of(head, visit)
            for part in range(2):
                scores = dot_nt(q_ref[rows_at(half), lanes_of(index, part)], keys)
                if visit >= 6:
                    scores = scores + bias[visit - 6]
                s_scr[slot, visit, part] = scores
                folded = fold(jnp.maximum, scores)
                if visit < 6:
                    folded = folded + seen[visit]
                if isinstance(half, int):
                    known = tops.get((half, part))
                    tops[half, part] = folded if known is None else jnp.maximum(known, folded)
                else:
                    row_max[slot, half, part] = jnp.maximum(row_max[slot, half, part], folded)

        def end():
            for half in range(2):
                for part in range(2):
                    top = jnp.maximum(row_max[slot, half, part], tops[half, part])
                    row_max[slot, half, part] = jnp.broadcast_to(
                        jnp.max(top, axis=1, keepdims=True), (HALF, HALF)
                    )

        return start, score, end

    def attend_steps(head, tile):
        index = head * TILES + tile
        slot = tile % 2
        kept = {}
        ones = jnp.ones((PAIR, HALF), BF16)

        def start():
            o_fold[...] = jnp.zeros(o_fold.shape, F32)

        def attend(visit):
            half = half_of(visit)
            values = jnp.concatenate([values_of(head, visit), ones], axis=1)
            for part in range(2):
                top = row_max[slot, half, part]
                if visit < 6:
                    top = top - seen[visit]
                probs = jnp.exp2((s_scr[slot, visit, part] - wide(top)) * SCALE_LOG2).astype(BF16)
                p_scr[visit, tile, part * HALF : (part + 1) * HALF, :] = probs
                if isinstance(half, int):
                    kept.setdefault((half, part), []).append((probs, values))
                else:
                    o_fold[half, part] = o_fold[half, part] + dot(probs, values)

        def end():
            for half in range(2):
                rows = slice(half * HALF, (half + 1) * HALF)
                for part in range(2):
                    probs = jnp.concatenate([pair[0] for pair in kept[half, part]], axis=1)
                    values = jnp.concatenate([pair[1] for pair in kept[half, part]], axis=0)
                    both = dot(probs, values) + o_fold[half, part]
                    inverse = 1.0 / both[:, HEAD_DIM:]
                    place = slice(tile * PAIR + part * HALF, tile * PAIR + (part + 1) * HALF)
                    inverses[half, place, :] = inverse
                    out = (both[:, :HEAD_DIM] * inverse).astype(BF16)
                    o_ref[rows, lanes_of(index, part)] = out
                    product = dout[rows, lanes_of(index, part)].astype(F32) * out.astype(F32)
                    delta[half, place, :] = jnp.broadcast_to(
                        jnp.sum(product, axis=1, keepdims=True), (HALF, HALF)
                    )
                    turned = inverse.T
                    lanes = slice(part * HALF, (part + 1) * HALF)
                    qt_scaled[half, tile, :, lanes] = (q_t[index, half, :, lanes].astype(F32) * turned).astype(BF16)
                    dt_scaled[half, tile, :, lanes] = (d_t[index, half, :, lanes].astype(F32) * turned).astype(BF16)

        return start, attend, end

    def forward_step(head, score_tile, attend_tile):
        running = []
        if score_tile is not None:
            running.append(score_steps(head, score_tile))
        if attend_tile is not None:
            running.append(attend_steps(head, attend_tile))
        for steps in running:
            steps[0]()
        for visit in FORWARD_ORDER:
            for steps in running:
                steps[1](visit)
        for steps in running:
            steps[2]()

    def backward_visits(head, visits):
        steps = [(visit, tile) for visit in visits for tile in range(TILES)]
        dprobs = {}

        def begin(step):
            visit, tile = step
            index = head * TILES + tile
            values = values_of(head, visit)
            rows = rows_at(half_of(visit))
            dprobs[step] = [dot_nt(dout[rows, lanes_of(index, part)], values) for part in range(2)]

        begin(steps[0])
        parity = lax.rem(head, 3)
        for number, step in enumerate(steps):
            if number + 1 < len(steps):
                begin(steps[number + 1])
            visit, tile = step
            half = half_of(visit)
            keys = keys_of(head, visit)
            halves = []
            for part in range(2):
                place = slice(tile * PAIR + part * HALF, tile * PAIR + (part + 1) * HALF)
                probs = p_scr[visit, tile, part * HALF : (part + 1) * HALF, :]
                dscore = probs.astype(F32) * (dprobs[step][part] - wide(delta[half, place, :]))
                dscore = dscore.astype(BF16)
                halves.append(dscore)
                dq_acc[half, place, :] = dq_acc[half, place, :] + dot(dscore, keys)
            dk_part = dot(qt_scaled[half, tile], jnp.concatenate(halves, axis=0))
            dv_part = dot(dt_scaled[half, tile], p_scr[visit, tile])
            dkey = dk_part if tile == 0 else dkey + dk_part
            dvalue = dv_part if tile == 0 else dvalue + dv_part
            if tile == TILES - 1:
                pair, side = pairs[visit], key_half(visit)
                acc[parity, pair, side, 0:HEAD_DIM] = acc[parity, pair, side, 0:HEAD_DIM] + dkey
                acc[parity, pair, side, HEAD_DIM : 2 * HEAD_DIM] = (
                    acc[parity, pair, side, HEAD_DIM : 2 * HEAD_DIM] + dvalue
                )

    def close_head(head):
        for tile in range(TILES):
            index = head * TILES + tile
            tile_rows = slice(tile * PAIR, (tile + 1) * PAIR)
            for half in range(2):
                result = (
                    dq_acc[half, tile_rows, :] * (inverses[half, tile_rows, :] * (inverse_mean[0:1, :] * SCALE))
                ).astype(BF16)
                rows = slice(half * HALF, (half + 1) * HALF)
                dq_ref[rows, lanes_of(index, 0)] = result[:HALF]
                dq_ref[rows, lanes_of(index, 1)] = result[HALF:]

    def first_copy(head, way):
        return remote(
            first_out.at[head, way],
            first_in.at[head, way],
            first_send.at[head, way],
            first_recv.at[head, way],
            sides[way],
        )

    def second_copy(head, way):
        return remote(
            second_out.at[head, way],
            second_in.at[head, way],
            second_send.at[head, way],
            second_recv.at[head, way],
            sides[way],
        )

    def last_copy(head):
        return remote(last_out.at[head], last_in.at[head], last_send.at[head], last_recv.at[head], partner_at)

    def cross_copy(head, pair):
        return remote(
            cross_out.at[head, pair],
            cross_in.at[head, pair],
            cross_send.at[head, pair],
            cross_recv.at[head, pair],
            partner_at,
        )

    def owed_copy(head, source, target):
        return remote(
            owed_out.at[head, target],
            owed_in.at[head, source],
            owed_send.at[head, target],
            owed_recv.at[head, source],
            at_member(target * 2 + odd),
        )

    def cross_start(head, pair):
        cross_out[head, pair] = acc[lax.rem(head, 3), pair, 1, :, other_rows].astype(BF16)
        cross_copy(head, pair).start()

    def scatter_1(head):
        for way in range(2):
            first_out[head, way] = acc[lax.rem(head, 3), across, 0, :, rows_of(way)].astype(BF16)
            first_copy(head, way).start()
        when(half_me < 2, cross_start, head, across)

    def scatter_2(head):
        when(half_me < 3, cross_start, head, right)
        when(half_me == 0, cross_start, head, left)

    def scatter_3(head):
        parity = lax.rem(head, 3)
        for way, pair in ((0, left), (1, right)):
            first_copy(head, way).wait_recv()
            mixed = acc[parity, pair, 0, :, rows_of(way)] + first_in[head, way].astype(F32)
            second_out[head, way, :, rows_of(way)] = mixed.astype(BF16)
            second_out[head, way, :, rows_of(1 - way)] = acc[parity, pair, 0, :, rows_of(1 - way)].astype(BF16)
            second_copy(head, way).start()

    def scatter_4(head):
        def pay(pair):
            cross_copy(head, pair).wait_recv()
            total = acc[lax.rem(head, 3), pair, 1, :, own_rows] + cross_in[head, pair].astype(F32)
            owed_out[head, pair] = total.astype(BF16)
            owed_copy(head, half_me, pair).start()

        for pair in (1, 2, 3):
            when(pair > half_me, pay, pair)

    def scatter_5(head):
        parity = lax.rem(head, 3)
        second_copy(head, 0).wait_recv()
        second_copy(head, 1).wait_recv()
        acc[parity, half_me, 0] = acc[parity, half_me, 0] + (
            second_in[head, 0].astype(F32) + second_in[head, 1].astype(F32)
        )
        last_out[head] = acc[parity, half_me, 0, :, other_rows].astype(BF16)
        last_copy(head).start()

    def scatter_6(head):
        parity = lax.rem(head, 3)
        lanes = pl.ds(pl.multiple_of(head * HEAD_DIM, HEAD_DIM), HEAD_DIM)

        def settle(side, total):
            rows = slice(side * HALF, (side + 1) * HALF)
            scale = inverse_mean[0:1, :]
            dk_ref[rows, lanes] = (total[:HEAD_DIM] * (scale * SCALE)).T.astype(BF16)
            dv_ref[rows, lanes] = (total[HEAD_DIM:] * scale).T.astype(BF16)

        def collect(source):
            owed_copy(head, source, half_me).wait_recv()
            acc[parity, half_me, 1, :, own_rows] = acc[parity, half_me, 1, :, own_rows] + owed_in[
                head, source
            ].astype(F32)

        for source in (0, 1, 2):
            when(source < half_me, collect, source)
        cross_copy(head, half_me).wait_recv()
        settle(1, acc[parity, half_me, 1, :, own_rows] + cross_in[head, half_me].astype(F32))
        last_copy(head).wait_recv()
        settle(0, acc[parity, half_me, 0, :, own_rows] + last_in[head].astype(F32))

    def scatter_end(head):
        first_copy(head, 0).wait_send()
        first_copy(head, 1).wait_send()
        second_copy(head, 0).wait_send()
        second_copy(head, 1).wait_send()
        last_copy(head).wait_send()
        for pair in range(4):
            when(pair >= half_me, lambda: cross_copy(head, pair).wait_send())
        for pair in (1, 2, 3):
            when(pair > half_me, lambda: owed_copy(head, half_me, pair).wait_send())

    def head_step(head, carry):
        gather_4(head)
        acc[lax.rem(head, 3)] = jnp.zeros(acc.shape[1:], F32)
        dq_acc[...] = jnp.zeros(dq_acc.shape, F32)
        earlier = head > 0

        first = head == 0

        second = head == 1
        third = head == 2
        forward_step(head, 0, None)
        when(first, gather_1, 1)
        when(third, gather_3, 3)
        when(first, weights_1)
        forward_step(head, 1, 0)
        when(first, gather_0, 2)
        when(second, gather_3, 2)
        when(first, weights_2)
        forward_step(head, 2, 1)
        when(first, gather_2, 1)
        when(second, gather_1, 3)
        when(head > 1, scatter_6, head - 2)
        when(first, weights_3)
        forward_step(head, 3, 2)
        when(earlier, scatter_4, head - 1)
        forward_step(head, None, 3)
        save_out(head).start()
        when(first, gather_1, 2)
        backward_visits(head, (0, 1))
        scatter_1(head)
        when(first, gather_3, 1)
        when(second, gather_2, 3)
        backward_visits(head, (2, 3, 4, 5))
        scatter_2(head)
        when(first, gather_0, 3)
        when(earlier, scatter_5, head - 1)
        backward_visits(head, (6, 7, 8))
        cross_start(head, half_me)
        scatter_3(head)
        when(first, gather_2, 2)
        close_head(head)
        save_dquery(head).start()
        when(head < KV_HEADS - 1, prepare, head + 1)
        return carry

    lax.fori_loop(0, KV_HEADS, head_step, 0)
    scatter_4(KV_HEADS - 1)
    scatter_6(KV_HEADS - 2)
    scatter_5(KV_HEADS - 1)
    scatter_6(KV_HEADS - 1)

    def finish(head, carry):
        gather_end(head)
        scatter_end(head)
        save_out(head).wait()
        save_dquery(head).wait()
        return carry

    lax.fori_loop(0, KV_HEADS, finish, 0)


CHUNKS = 4


def carry_kernel(count, *refs):
    sources, targets, slots = refs[:count], refs[count : 2 * count], refs[2 * count : 3 * count]
    sem = refs[3 * count]

    def copies(number, chunk):
        rows = sources[number].shape[0] // CHUNKS
        place = pl.ds(chunk * rows, rows)
        arrive = pltpu.make_async_copy(
            sources[number].at[place], slots[number].at[place], sem.at[0, number, chunk]
        )
        leave = pltpu.make_async_copy(
            slots[number].at[place], targets[number].at[place], sem.at[1, number, chunk]
        )
        return arrive, leave

    steps = [copies(number, chunk) for chunk in range(CHUNKS) for number in range(count)]
    for arrive, _ in steps:
        arrive.start()
    for arrive, leave in steps:
        arrive.wait()
        leave.start()
    for _, leave in steps:
        leave.wait()


def carry_out(*arrays):
    hbm = pl.BlockSpec(memory_space=pl.ANY)
    count = len(arrays)
    return pl.pallas_call(
        functools.partial(carry_kernel, count),
        out_shape=tuple(jax.ShapeDtypeStruct(array.shape, array.dtype) for array in arrays),
        in_specs=[hbm] * count,
        out_specs=(hbm,) * count,
        scratch_shapes=[pltpu.VMEM(array.shape, array.dtype) for array in arrays]
        + [pltpu.SemaphoreType.DMA((2, count, CHUNKS))],
        compiler_params=pltpu.CompilerParams(vmem_limit_bytes=56 * 1024 * 1024),
    )(*arrays)


def on_device(n_dp, n_blocks, queries, key_states, value_states, grad_out, token_weight, span_size, short_lengths):
    vmem = pl.BlockSpec(memory_space=pltpu.VMEM)
    smem = pl.BlockSpec(memory_space=pltpu.SMEM)
    hbm = pl.BlockSpec(memory_space=pl.ANY)
    wide = jax.ShapeDtypeStruct((ROWS_DEV, HEADS * HEAD_DIM), BF16)
    narrow = jax.ShapeDtypeStruct((ROWS_DEV, KV_HEADS * HEAD_DIM), BF16)
    all_rows = (2, TILES * PAIR, HEAD_DIM)
    results = pl.pallas_call(
        functools.partial(kernel, n_dp, n_blocks),
        out_shape=(wide, wide, narrow, narrow),
        in_specs=[hbm, vmem, vmem, hbm, vmem, smem, smem],
        out_specs=(hbm, hbm, vmem, vmem),
        scratch_shapes=[
            pltpu.VMEM((ROWS_DEV, HEADS * HEAD_DIM), BF16),
            pltpu.VMEM((ROWS_DEV, HEADS * HEAD_DIM), BF16),
            pltpu.VMEM((ROWS_DEV, HEADS * HEAD_DIM), BF16),
            pltpu.VMEM((ROWS_DEV, HEADS * HEAD_DIM), BF16),
            pltpu.VMEM((KV_HEADS, 4, 2, PAIR, 2 * HEAD_DIM), BF16),
            pltpu.VMEM((KV_HEADS, 2, 2 * HEAD_DIM, HALF), BF16),
            pltpu.VMEM((KV_HEADS, 2, 2 * HEAD_DIM, HALF), BF16),
            pltpu.VMEM((KV_HEADS, 2, 2 * HEAD_DIM, PAIR), BF16),
            pltpu.VMEM((KV_HEADS, 2, 2 * HEAD_DIM, PAIR), BF16),
            pltpu.VMEM((KV_HEADS, 2 * HEAD_DIM, HALF), BF16),
            pltpu.VMEM((KV_HEADS, 2 * HEAD_DIM, HALF), BF16),
            pltpu.VMEM((KV_HEADS, 4, 2 * HEAD_DIM, HALF), BF16),
            pltpu.VMEM((KV_HEADS, 4, 2 * HEAD_DIM, HALF), BF16),
            pltpu.VMEM((KV_HEADS, 4, 2 * HEAD_DIM, HALF), BF16),
            pltpu.VMEM((KV_HEADS, 4, 2 * HEAD_DIM, HALF), BF16),
            pltpu.VMEM((HEADS // 2, 2, HEAD_DIM, PAIR), BF16),
            pltpu.VMEM((HEADS // 2, 2, HEAD_DIM, PAIR), BF16),
            pltpu.VMEM((ROWS_DEV, HEADS * HEAD_DIM), BF16),
            pltpu.VMEM((3, HALF, PAIR), F32),
            pltpu.VMEM((2, VISITS, 2, HALF, PAIR), F32),
            pltpu.VMEM((VISITS, TILES, PAIR, PAIR), BF16),
            pltpu.VMEM((3, 4, 2, 2 * HEAD_DIM, PAIR), F32),
            pltpu.VMEM((2, 2, 2, HALF, HALF), F32),
            pltpu.VMEM((2, 2, HALF, PAIR), F32),
            pltpu.VMEM(all_rows, F32),
            pltpu.VMEM(all_rows, F32),
            pltpu.VMEM(all_rows, F32),
            pltpu.VMEM((2, TILES, HEAD_DIM, PAIR), BF16),
            pltpu.VMEM((2, TILES, HEAD_DIM, PAIR), BF16),
            pltpu.VMEM((SPAN_MAX, 8, 128), F32),
            pltpu.VMEM((n_dp, 8, 128), F32),
            pltpu.VMEM((n_blocks, 8, 128), F32),
            pltpu.VMEM((8, 128), F32),
            pltpu.SemaphoreType.DMA((2, KV_HEADS)),
            pltpu.SemaphoreType.DMA((2, KV_HEADS)),
            pltpu.SemaphoreType.DMA((KV_HEADS,)),
            pltpu.SemaphoreType.DMA((KV_HEADS,)),
            pltpu.SemaphoreType.DMA((KV_HEADS, 2, 2)),
            pltpu.SemaphoreType.DMA((KV_HEADS, 2, 2)),
            pltpu.SemaphoreType.DMA((KV_HEADS, 2)),
            pltpu.SemaphoreType.DMA((KV_HEADS, 2)),
            pltpu.SemaphoreType.DMA((KV_HEADS, 4)),
            pltpu.SemaphoreType.DMA((KV_HEADS, 4)),
            pltpu.SemaphoreType.DMA((KV_HEADS, 4)),
            pltpu.SemaphoreType.DMA((KV_HEADS, 4)),
            pltpu.SemaphoreType.DMA((KV_HEADS, 2)),
            pltpu.SemaphoreType.DMA((KV_HEADS, 2)),
            pltpu.SemaphoreType.DMA((KV_HEADS, 2)),
            pltpu.SemaphoreType.DMA((KV_HEADS, 2)),
            pltpu.SemaphoreType.DMA((KV_HEADS,)),
            pltpu.SemaphoreType.DMA((KV_HEADS,)),
            pltpu.SemaphoreType.DMA((KV_HEADS, 4)),
            pltpu.SemaphoreType.DMA((KV_HEADS, 4)),
            pltpu.SemaphoreType.DMA((KV_HEADS, 4)),
            pltpu.SemaphoreType.DMA((KV_HEADS, 4)),
            pltpu.SemaphoreType.DMA((24,)),
            pltpu.SemaphoreType.DMA((24,)),
        ],
        compiler_params=pltpu.CompilerParams(
            collective_id=0, has_side_effects=True, vmem_limit_bytes=56 * 1024 * 1024
        ),
    )(
        queries,
        key_states,
        value_states,
        grad_out,
        token_weight.reshape(1, ROWS_DEV),
        span_size,
        jnp.swapaxes(short_lengths, 1, 2),
    )
    return carry_out(*results)


def solution(mesh):
    rows = P(("dp", "cp"), None)
    n_dp = mesh.shape["dp"]
    n_blocks = mesh.shape["cp"] // SPAN_MAX
    return jax.shard_map(
        functools.partial(on_device, n_dp, n_blocks),
        mesh=mesh,
        in_specs=(rows, rows, rows, rows, P(("dp", "cp")), P("dp", None), P("dp", None, None)),
        out_specs=(rows, rows, rows, rows),
        check_vma=False,
    )
```

```python
import functools

import jax
import jax.numpy as jnp
from jax import lax
from jax.experimental import pallas as pl
from jax.experimental.pallas import tpu as pltpu
from jax.sharding import PartitionSpec as P

HEADS = 32
KV_HEADS = 4
HEAD_DIM = 128
SPAN_MAX = 8
HALF = 128
ROWS_DEV = 256
SLOTS = 8
GROUPS = HEADS // KV_HEADS
TILES = GROUPS // 2
PAIR = 256
VISITS = 9
FORWARD_ORDER = (1, 3, 5, 0, 2, 4, 6, 7, 8)
NEG = -1e30
SCALE = HEAD_DIM**-0.5
SCALE_LOG2 = SCALE * 1.4426950408889634
F32 = jnp.float32
BF16 = jnp.bfloat16


def dot(a, b):
    return lax.dot_general(a, b, (((1,), (0,)), ((), ())), preferred_element_type=F32)


def dot_nt(a, b):
    return lax.dot_general(a, b, (((1,), (1,)), ((), ())), preferred_element_type=F32)


def kernel(
    n_dp,
    n_blocks,
    q_hbm,
    k_ref,
    v_ref,
    g_hbm,
    w_ref,
    span_ref,
    len_ref,
    o_hbm,
    dq_hbm,
    dk_ref,
    dv_ref,
    q_ref,
    g_ref,
    o_ref,
    dq_ref,
    kv,
    first_out,
    first_in,
    second_out,
    second_in,
    last_out,
    last_in,
    cross_out,
    cross_in,
    owed_out,
    owed_in,
    q_t,
    d_t,
    dout,
    bias,
    s_scr,
    p_scr,
    acc,
    row_max,
    o_fold,
    dq_acc,
    delta,
    inverses,
    qt_scaled,
    dt_scaled,
    sum_block,
    sum_dp,
    sum_y,
    inverse_mean,
    in_sem,
    out_sem,
    z_send,
    z_recv,
    near_send,
    near_recv,
    far_send,
    far_recv,
    up_send,
    up_recv,
    turn_send,
    turn_recv,
    first_send,
    first_recv,
    second_send,
    second_recv,
    last_send,
    last_recv,
    cross_send,
    cross_recv,
    owed_send,
    owed_recv,
    w_send,
    w_recv,
):
    dp = lax.axis_index("dp")
    cp = lax.axis_index("cp")
    me = lax.rem(cp, SPAN_MAX)
    block = lax.div(cp, SPAN_MAX)
    base = block * SPAN_MAX
    half_me = lax.div(me, 2)
    odd = lax.rem(me, 2)

    def peer_of(step):
        return lax.rem(me + step, SPAN_MAX)

    def at_member(member):
        return (dp, base + member)

    def at_dp(step):
        return (lax.rem(dp + step, n_dp), cp)

    def at_block(step):
        return (dp, lax.rem(block + step, n_blocks) * SPAN_MAX + me)

    barrier = pltpu.get_barrier_semaphore()
    partners = [at_member(peer_of(step)) for step in range(1, SPAN_MAX)]
    partners += [at_dp(step) for step in range(1, n_dp)]
    partners += [at_block(step) for step in range(1, n_blocks)]
    for partner in partners:
        pl.semaphore_signal(barrier, inc=1, device_id=partner, device_id_type=pl.DeviceIdType.MESH)

    across = lax.rem(half_me + 2, 4)
    left = lax.rem(half_me + 3, 4)
    right = lax.rem(half_me + 1, 4)
    own_rows = pl.ds(pl.multiple_of(odd * HALF, HALF), HALF)
    other_rows = pl.ds(pl.multiple_of((1 - odd) * HALF, HALF), HALF)

    def head_lanes(head):
        width = GROUPS * HEAD_DIM
        return pl.ds(pl.multiple_of(head * width, width), width)

    def load_queries(head):
        return pltpu.make_async_copy(
            q_hbm.at[:, head_lanes(head)], q_ref.at[:, head_lanes(head)], in_sem.at[0, head]
        )

    def load_grads(head):
        return pltpu.make_async_copy(
            g_hbm.at[:, head_lanes(head)], g_ref.at[:, head_lanes(head)], in_sem.at[1, head]
        )

    def save_out(head):
        return pltpu.make_async_copy(
            o_ref.at[:, head_lanes(head)], o_hbm.at[:, head_lanes(head)], out_sem.at[0, head]
        )

    def save_dquery(head):
        return pltpu.make_async_copy(
            dq_ref.at[:, head_lanes(head)], dq_hbm.at[:, head_lanes(head)], out_sem.at[1, head]
        )

    for head in range(KV_HEADS):
        load_queries(head).start()
        load_grads(head).start()

    for head in range(KV_HEADS):
        lanes = slice(head * HEAD_DIM, (head + 1) * HEAD_DIM)
        for half in range(2):
            rows = slice(half * HALF, (half + 1) * HALF)
            kv[head, half_me, half, own_rows, 0:HEAD_DIM] = k_ref[rows, lanes]
            kv[head, half_me, half, own_rows, HEAD_DIM : 2 * HEAD_DIM] = v_ref[rows, lanes]

    weight_part = jnp.sum(w_ref[...], axis=1, keepdims=True)
    sum_block[me] = jnp.broadcast_to(weight_part, (8, 128))

    pl.semaphore_wait(barrier, len(partners))

    def remote(src, dst, send_sem, recv_sem, target):
        return pltpu.make_async_remote_copy(
            src_ref=src,
            dst_ref=dst,
            send_sem=send_sem,
            recv_sem=recv_sem,
            device_id=target,
            device_id_type=pl.DeviceIdType.MESH,
        )

    def weight_copy(buffer, slot, offset, step, target, source_slot):
        return remote(
            buffer.at[slot],
            buffer.at[slot],
            w_send.at[offset + step - 1],
            w_recv.at[offset + source_slot],
            target,
        )

    def send_weights(buffer, slot, count, offset, targets):
        for step in range(1, count):
            weight_copy(buffer, slot, offset, step, targets(step), slot).start()

    def wait_weights(buffer, slot, count, offset, targets):
        for step in range(1, count):
            source = lax.rem(slot + step, count)
            weight_copy(buffer, source, offset, step, targets(step), source).wait_recv()
            weight_copy(buffer, slot, offset, step, targets(step), slot).wait_send()
        total = buffer[0]
        for slot_index in range(1, count):
            total = total + buffer[slot_index]
        return total

    partner_at = at_member(lax.bitwise_xor(me, 1))
    left_at = at_member(left * 2 + odd)
    right_at = at_member(right * 2 + odd)

    def rows_of(item):
        return own_rows if item == 0 else other_rows

    def when(condition, step, *given):
        @pl.when(condition)
        def _():
            step(*given)

    sides = (left_at, right_at)

    def partner_copy(head):
        view = kv.at[head, half_me, 0, own_rows]
        return remote(view, view, z_send.at[head], z_recv.at[head], partner_at)

    def near_copy(head, item, way, pair):
        view = kv.at[head, pair, 0, rows_of(item)]
        return remote(view, view, near_send.at[head, item, way], near_recv.at[head, item, way], sides[way])

    def far_copy(head, item, pair):
        view = kv.at[head, pair, 0, rows_of(item)]
        return remote(view, view, far_send.at[head, item], far_recv.at[head, item], sides[1 - item])

    def upper_copy(head, source, target):
        view = kv.at[head, source, 1, own_rows]
        return remote(
            view, view, up_send.at[head, target], up_recv.at[head, source], at_member(target * 2 + odd)
        )

    def turned_copy(head, pair, item):
        view = kv.at[head, pair, 1, rows_of(item)]
        return remote(view, view, turn_send.at[head, pair], turn_recv.at[head, pair], partner_at)

    def gather_0(head):
        partner_copy(head).start()
        near_copy(head, 0, 0, half_me).start()
        near_copy(head, 0, 1, half_me).start()
        for target in (0, 1, 2):
            when(target < half_me, lambda: upper_copy(head, half_me, target).start())
        turned_copy(head, half_me, 0).start()

    def gather_1(head):
        partner_copy(head).wait_recv()
        near_copy(head, 1, 0, half_me).start()
        near_copy(head, 1, 1, half_me).start()

    def gather_2(head):
        near_copy(head, 0, 1, left).wait_recv()
        far_copy(head, 0, left).start()
        near_copy(head, 0, 0, right).wait_recv()

    def gather_turn(head):
        def turn_on(pair):
            upper_copy(head, pair, half_me).wait_recv()
            turned_copy(head, pair, 0).start()

        for pair in (1, 2, 3):
            when(pair > half_me, turn_on, pair)

    def gather_forward(head):
        near_copy(head, 1, 0, right).wait_recv()
        far_copy(head, 1, right).start()
        near_copy(head, 1, 1, left).wait_recv()

    def gather_3(head):
        gather_turn(head)
        gather_forward(head)

    def gather_4(head):
        for pair in range(4):
            when(pair >= half_me, lambda: turned_copy(head, pair, 1).wait_recv())
        far_copy(head, 0, across).wait_recv()
        far_copy(head, 1, across).wait_recv()

    def gather_end(head):
        partner_copy(head).wait_send()
        for item in range(2):
            near_copy(head, item, 0, half_me).wait_send()
            near_copy(head, item, 1, half_me).wait_send()
            far_copy(head, item, (left, right)[item]).wait_send()
        for target in (0, 1, 2):
            when(target < half_me, lambda: upper_copy(head, half_me, target).wait_send())
        for pair in range(4):
            when(pair >= half_me, lambda: turned_copy(head, pair, 0).wait_send())

    gather_0(0)
    send_weights(sum_block, me, SPAN_MAX, 0, lambda step: at_member(peer_of(step)))

    span = span_ref[0, cp]
    spread = span > 1
    row_id = lax.broadcasted_iota(jnp.int32, (HALF, HALF), 0)
    col_id = lax.broadcasted_iota(jnp.int32, (HALF, HALF), 1)
    slot_of = {}
    for name, ids in (("q0", row_id), ("q1", row_id + HALF), ("k0", col_id), ("k1", col_id + HALF)):
        slot_count = jnp.zeros((HALF, HALF), jnp.int32)
        end = jnp.int32(0)
        for slot in range(SLOTS):
            end = end + len_ref[0, slot, cp]
            slot_count = slot_count + (ids >= end).astype(jnp.int32)
        slot_of[name] = slot_count
    spread_add = jnp.where(spread, 1, 0)

    def same_document(q_name, k_name):
        equal = (slot_of[q_name] == slot_of[k_name]).astype(jnp.int32) + spread_add
        return jnp.where(equal > 0, 0.0, NEG)

    causal = jnp.where(col_id <= row_id, 0.0, NEG)
    own_lower = jnp.minimum(same_document("q0", "k0"), causal)
    own_upper = jnp.minimum(same_document("q1", "k1"), causal)
    own_cross = same_document("q1", "k0")

    partner_seen = jnp.where(span > 1, 0.0, NEG)
    for side in range(2):
        lanes = slice(side * HALF, (side + 1) * HALF)
        is_me = jnp.where(odd == side, 1, 0) + jnp.zeros((HALF, HALF), jnp.int32) > 0
        after = jnp.where(odd > side, 0.0, NEG)
        before = jnp.where(odd < side, 0.0, NEG)
        bias[0, :, lanes] = jnp.where(is_me, own_cross, partner_seen)
        bias[1, :, lanes] = jnp.where(is_me, own_lower, jnp.minimum(partner_seen, after))
        bias[2, :, lanes] = jnp.where(is_me, own_upper, jnp.minimum(partner_seen, before))
    seen = {}
    for visit, pair_step in ((0, 2), (2, 3), (4, 1)):
        other = lax.rem(half_me + pair_step, 4) * 2
        seen[visit] = seen[visit + 1] = jnp.where(lax.bitwise_xor(other, me) < span, 0.0, NEG)

    gather_1(0)
    gather_turn(0)
    gather_2(0)
    gather_0(1)
    gather_forward(0)

    def prepare(head):
        load_queries(head).wait()
        load_grads(head).wait()
        scaled = [jnp.broadcast_to(w_ref[0:1, half * HALF : (half + 1) * HALF], (HALF, HALF)).T for half in range(2)]

        def turn(tile, carry):
            index = head * TILES + tile
            for part in range(2):
                lanes = pl.ds(pl.multiple_of((index * 2 + part) * HEAD_DIM, HEAD_DIM), HEAD_DIM)
                columns = slice(part * HALF, (part + 1) * HALF)
                for half in range(2):
                    rows = slice(half * HALF, (half + 1) * HALF)
                    q_t[index, half, :, columns] = q_ref[rows, lanes].T
                    weighted = (g_ref[rows, lanes].astype(F32) * scaled[half]).astype(BF16)
                    dout[rows, lanes] = weighted
                    d_t[index, half, :, columns] = weighted.T
            return carry

        lax.fori_loop(0, TILES, turn, 0)

    prepare(0)

    def weights_1():
        sum_dp[dp] = wait_weights(sum_block, me, SPAN_MAX, 0, lambda step: at_member(peer_of(step)))
        send_weights(sum_dp, dp, n_dp, 8, at_dp)

    def weights_2():
        sum_y[block] = wait_weights(sum_dp, dp, n_dp, 8, at_dp)
        send_weights(sum_y, block, n_blocks, 16, at_block)

    def weights_3():
        rows_total = ROWS_DEV * SPAN_MAX * n_dp * n_blocks
        inverse_mean[...] = rows_total / wait_weights(sum_y, block, n_blocks, 16, at_block)

    pairs = (across, across, left, left, right, right, half_me, half_me, half_me)

    def half_of(visit):
        if visit in (1, 3, 5):
            return jnp.where(pairs[visit] < half_me, 0, 1)
        return 0 if visit == 7 else 1

    def key_half(visit):
        if visit in (1, 3, 5):
            return jnp.where(pairs[visit] < half_me, 0, 1)
        return 1 if visit == 8 else 0

    def lanes_of(index, part):
        return pl.ds(pl.multiple_of((index * 2 + part) * HEAD_DIM, HEAD_DIM), HEAD_DIM)

    def rows_at(half):
        if isinstance(half, int):
            return pl.ds(half * HALF, HALF)
        return pl.ds(pl.multiple_of(half * HALF, HALF), HALF)

    def keys_of(head, visit):
        return kv[head, pairs[visit], key_half(visit), :, 0:HEAD_DIM]

    def values_of(head, visit):
        return kv[head, pairs[visit], key_half(visit), :, HEAD_DIM : 2 * HEAD_DIM]

    def fold(op, block):
        return op(block[:, :HALF], block[:, HALF:])

    def wide(block):
        return jnp.concatenate([block, block], axis=1)

    def score_steps(head, tile):
        index = head * TILES + tile
        slot = tile % 2
        tops = {}

        def start():
            row_max[slot] = jnp.full(row_max.shape[1:], NEG, F32)

        def score(visit):
            half = half_of(visit)
            keys = keys_of(head, visit)
            for part in range(2):
                scores = dot_nt(q_ref[rows_at(half), lanes_of(index, part)], keys)
                if visit >= 6:
                    scores = scores + bias[visit - 6]
                s_scr[slot, visit, part] = scores
                folded = fold(jnp.maximum, scores)
                if visit < 6:
                    folded = folded + seen[visit]
                if isinstance(half, int):
                    known = tops.get((half, part))
                    tops[half, part] = folded if known is None else jnp.maximum(known, folded)
                else:
                    row_max[slot, half, part] = jnp.maximum(row_max[slot, half, part], folded)

        def end():
            for half in range(2):
                for part in range(2):
                    top = jnp.maximum(row_max[slot, half, part], tops[half, part])
                    row_max[slot, half, part] = jnp.broadcast_to(
                        jnp.max(top, axis=1, keepdims=True), (HALF, HALF)
                    )

        return start, score, end

    def attend_steps(head, tile):
        index = head * TILES + tile
        slot = tile % 2
        kept = {}
        ones = jnp.ones((PAIR, HALF), BF16)

        def start():
            o_fold[...] = jnp.zeros(o_fold.shape, F32)

        def attend(visit):
            half = half_of(visit)
            values = jnp.concatenate([values_of(head, visit), ones], axis=1)
            for part in range(2):
                top = row_max[slot, half, part]
                if visit < 6:
                    top = top - seen[visit]
                probs = jnp.exp2((s_scr[slot, visit, part] - wide(top)) * SCALE_LOG2).astype(BF16)
                p_scr[visit, tile, part * HALF : (part + 1) * HALF, :] = probs
                if isinstance(half, int):
                    kept.setdefault((half, part), []).append((probs, values))
                else:
                    o_fold[half, part] = o_fold[half, part] + dot(probs, values)

        def end():
            for half in range(2):
                rows = slice(half * HALF, (half + 1) * HALF)
                for part in range(2):
                    probs = jnp.concatenate([pair[0] for pair in kept[half, part]], axis=1)
                    values = jnp.concatenate([pair[1] for pair in kept[half, part]], axis=0)
                    both = dot(probs, values) + o_fold[half, part]
                    inverse = 1.0 / both[:, HEAD_DIM:]
                    place = slice(tile * PAIR + part * HALF, tile * PAIR + (part + 1) * HALF)
                    inverses[half, place, :] = inverse
                    out = (both[:, :HEAD_DIM] * inverse).astype(BF16)
                    o_ref[rows, lanes_of(index, part)] = out
                    product = dout[rows, lanes_of(index, part)].astype(F32) * out.astype(F32)
                    delta[half, place, :] = jnp.broadcast_to(
                        jnp.sum(product, axis=1, keepdims=True), (HALF, HALF)
                    )
                    turned = inverse.T
                    lanes = slice(part * HALF, (part + 1) * HALF)
                    qt_scaled[half, tile, :, lanes] = (q_t[index, half, :, lanes].astype(F32) * turned).astype(BF16)
                    dt_scaled[half, tile, :, lanes] = (d_t[index, half, :, lanes].astype(F32) * turned).astype(BF16)

        return start, attend, end

    def forward_step(head, score_tile, attend_tile):
        running = []
        if score_tile is not None:
            running.append(score_steps(head, score_tile))
        if attend_tile is not None:
            running.append(attend_steps(head, attend_tile))
        for steps in running:
            steps[0]()
        for visit in FORWARD_ORDER:
            for steps in running:
                steps[1](visit)
        for steps in running:
            steps[2]()

    def backward_visits(head, visits):
        steps = [(visit, tile) for visit in visits for tile in range(TILES)]
        dprobs = {}

        def begin(step):
            visit, tile = step
            index = head * TILES + tile
            values = values_of(head, visit)
            rows = rows_at(half_of(visit))
            dprobs[step] = [dot_nt(dout[rows, lanes_of(index, part)], values) for part in range(2)]

        begin(steps[0])
        parity = lax.rem(head, 3)
        for number, step in enumerate(steps):
            if number + 1 < len(steps):
                begin(steps[number + 1])
            visit, tile = step
            half = half_of(visit)
            keys = keys_of(head, visit)
            halves = []
            for part in range(2):
                place = slice(tile * PAIR + part * HALF, tile * PAIR + (part + 1) * HALF)
                probs = p_scr[visit, tile, part * HALF : (part + 1) * HALF, :]
                dscore = probs.astype(F32) * (dprobs[step][part] - wide(delta[half, place, :]))
                dscore = dscore.astype(BF16)
                halves.append(dscore)
                dq_acc[half, place, :] = dq_acc[half, place, :] + dot(dscore, keys)
            dk_part = dot(qt_scaled[half, tile], jnp.concatenate(halves, axis=0))
            dv_part = dot(dt_scaled[half, tile], p_scr[visit, tile])
            dkey = dk_part if tile == 0 else dkey + dk_part
            dvalue = dv_part if tile == 0 else dvalue + dv_part
            if tile == TILES - 1:
                pair, side = pairs[visit], key_half(visit)
                acc[parity, pair, side, 0:HEAD_DIM] = acc[parity, pair, side, 0:HEAD_DIM] + dkey
                acc[parity, pair, side, HEAD_DIM : 2 * HEAD_DIM] = (
                    acc[parity, pair, side, HEAD_DIM : 2 * HEAD_DIM] + dvalue
                )

    def close_head(head):
        for tile in range(TILES):
            index = head * TILES + tile
            tile_rows = slice(tile * PAIR, (tile + 1) * PAIR)
            for half in range(2):
                result = (
                    dq_acc[half, tile_rows, :] * (inverses[half, tile_rows, :] * (inverse_mean[0:1, :] * SCALE))
                ).astype(BF16)
                rows = slice(half * HALF, (half + 1) * HALF)
                dq_ref[rows, lanes_of(index, 0)] = result[:HALF]
                dq_ref[rows, lanes_of(index, 1)] = result[HALF:]

    def first_copy(head, way):
        return remote(
            first_out.at[head, way],
            first_in.at[head, way],
            first_send.at[head, way],
            first_recv.at[head, way],
            sides[way],
        )

    def second_copy(head, way):
        return remote(
            second_out.at[head, way],
            second_in.at[head, way],
            second_send.at[head, way],
            second_recv.at[head, way],
            sides[way],
        )

    def last_copy(head):
        return remote(last_out.at[head], last_in.at[head], last_send.at[head], last_recv.at[head], partner_at)

    def cross_copy(head, pair):
        return remote(
            cross_out.at[head, pair],
            cross_in.at[head, pair],
            cross_send.at[head, pair],
            cross_recv.at[head, pair],
            partner_at,
        )

    def owed_copy(head, source, target):
        return remote(
            owed_out.at[head, target],
            owed_in.at[head, source],
            owed_send.at[head, target],
            owed_recv.at[head, source],
            at_member(target * 2 + odd),
        )

    def cross_start(head, pair):
        cross_out[head, pair] = acc[lax.rem(head, 3), pair, 1, :, other_rows].astype(BF16)
        cross_copy(head, pair).start()

    def scatter_1(head):
        for way in range(2):
            first_out[head, way] = acc[lax.rem(head, 3), across, 0, :, rows_of(way)].astype(BF16)
            first_copy(head, way).start()
        when(half_me < 2, cross_start, head, across)

    def scatter_2(head):
        when(half_me < 3, cross_start, head, right)
        when(half_me == 0, cross_start, head, left)

    def scatter_3(head):
        parity = lax.rem(head, 3)
        for way, pair in ((0, left), (1, right)):
            first_copy(head, way).wait_recv()
            mixed = acc[parity, pair, 0, :, rows_of(way)] + first_in[head, way].astype(F32)
            second_out[head, way, :, rows_of(way)] = mixed.astype(BF16)
            second_out[head, way, :, rows_of(1 - way)] = acc[parity, pair, 0, :, rows_of(1 - way)].astype(BF16)
            second_copy(head, way).start()

    def scatter_4(head):
        def pay(pair):
            cross_copy(head, pair).wait_recv()
            total = acc[lax.rem(head, 3), pair, 1, :, own_rows] + cross_in[head, pair].astype(F32)
            owed_out[head, pair] = total.astype(BF16)
            owed_copy(head, half_me, pair).start()

        for pair in (1, 2, 3):
            when(pair > half_me, pay, pair)

    def scatter_5(head):
        parity = lax.rem(head, 3)
        second_copy(head, 0).wait_recv()
        second_copy(head, 1).wait_recv()
        acc[parity, half_me, 0] = acc[parity, half_me, 0] + (
            second_in[head, 0].astype(F32) + second_in[head, 1].astype(F32)
        )
        last_out[head] = acc[parity, half_me, 0, :, other_rows].astype(BF16)
        last_copy(head).start()

    def scatter_6(head):
        parity = lax.rem(head, 3)
        lanes = pl.ds(pl.multiple_of(head * HEAD_DIM, HEAD_DIM), HEAD_DIM)

        def settle(side, total):
            rows = slice(side * HALF, (side + 1) * HALF)
            scale = inverse_mean[0:1, :]
            dk_ref[rows, lanes] = (total[:HEAD_DIM] * (scale * SCALE)).T.astype(BF16)
            dv_ref[rows, lanes] = (total[HEAD_DIM:] * scale).T.astype(BF16)

        def collect(source):
            owed_copy(head, source, half_me).wait_recv()
            acc[parity, half_me, 1, :, own_rows] = acc[parity, half_me, 1, :, own_rows] + owed_in[
                head, source
            ].astype(F32)

        for source in (0, 1, 2):
            when(source < half_me, collect, source)
        cross_copy(head, half_me).wait_recv()
        settle(1, acc[parity, half_me, 1, :, own_rows] + cross_in[head, half_me].astype(F32))
        last_copy(head).wait_recv()
        settle(0, acc[parity, half_me, 0, :, own_rows] + last_in[head].astype(F32))

    def scatter_end(head):
        first_copy(head, 0).wait_send()
        first_copy(head, 1).wait_send()
        second_copy(head, 0).wait_send()
        second_copy(head, 1).wait_send()
        last_copy(head).wait_send()
        for pair in range(4):
            when(pair >= half_me, lambda: cross_copy(head, pair).wait_send())
        for pair in (1, 2, 3):
            when(pair > half_me, lambda: owed_copy(head, half_me, pair).wait_send())

    def head_step(head, carry):
        gather_4(head)
        acc[lax.rem(head, 3)] = jnp.zeros(acc.shape[1:], F32)
        dq_acc[...] = jnp.zeros(dq_acc.shape, F32)
        earlier = head > 0

        first = head == 0

        second = head == 1
        third = head == 2
        forward_step(head, 0, None)
        when(first, gather_1, 1)
        when(third, gather_3, 3)
        when(first, weights_1)
        forward_step(head, 1, 0)
        when(first, gather_0, 2)
        when(second, gather_3, 2)
        forward_step(head, 2, 1)
        when(first, gather_2, 1)
        when(second, gather_1, 3)
        when(head > 1, scatter_6, head - 2)
        forward_step(head, 3, 2)
        when(earlier, scatter_4, head - 1)
        forward_step(head, None, 3)
        save_out(head).start()
        when(first, gather_1, 2)
        when(first, weights_2)
        backward_visits(head, (0, 1))
        scatter_1(head)
        when(first, gather_3, 1)
        when(second, gather_2, 3)
        backward_visits(head, (2, 3, 4, 5))
        scatter_2(head)
        when(first, gather_0, 3)
        when(earlier, scatter_5, head - 1)
        backward_visits(head, (6, 7, 8))
        cross_start(head, half_me)
        scatter_3(head)
        when(first, gather_2, 2)
        when(first, weights_3)
        close_head(head)
        save_dquery(head).start()
        when(head < KV_HEADS - 1, prepare, head + 1)
        return carry

    lax.fori_loop(0, KV_HEADS, head_step, 0)
    scatter_4(KV_HEADS - 1)
    scatter_6(KV_HEADS - 2)
    scatter_5(KV_HEADS - 1)
    scatter_6(KV_HEADS - 1)

    def finish(head, carry):
        gather_end(head)
        scatter_end(head)
        save_out(head).wait()
        save_dquery(head).wait()
        return carry

    lax.fori_loop(0, KV_HEADS, finish, 0)


CHUNKS = 2


def carry_kernel(count, *refs):
    sources, targets, slots = refs[:count], refs[count : 2 * count], refs[2 * count : 3 * count]
    sem = refs[3 * count]

    def copies(number, chunk):
        rows = sources[number].shape[0] // CHUNKS
        place = pl.ds(chunk * rows, rows)
        arrive = pltpu.make_async_copy(
            sources[number].at[place], slots[number].at[place], sem.at[0, number, chunk]
        )
        leave = pltpu.make_async_copy(
            slots[number].at[place], targets[number].at[place], sem.at[1, number, chunk]
        )
        return arrive, leave

    steps = [copies(number, chunk) for chunk in range(CHUNKS) for number in range(count)]
    for arrive, _ in steps:
        arrive.start()
    for arrive, leave in steps:
        arrive.wait()
        leave.start()
    for _, leave in steps:
        leave.wait()


def carry_out(*arrays):
    hbm = pl.BlockSpec(memory_space=pl.ANY)
    count = len(arrays)
    return pl.pallas_call(
        functools.partial(carry_kernel, count),
        out_shape=tuple(jax.ShapeDtypeStruct(array.shape, array.dtype) for array in arrays),
        in_specs=[hbm] * count,
        out_specs=(hbm,) * count,
        scratch_shapes=[pltpu.VMEM(array.shape, array.dtype) for array in arrays]
        + [pltpu.SemaphoreType.DMA((2, count, CHUNKS))],
        compiler_params=pltpu.CompilerParams(vmem_limit_bytes=56 * 1024 * 1024),
    )(*arrays)


def on_device(n_dp, n_blocks, queries, key_states, value_states, grad_out, token_weight, span_size, short_lengths):
    vmem = pl.BlockSpec(memory_space=pltpu.VMEM)
    smem = pl.BlockSpec(memory_space=pltpu.SMEM)
    hbm = pl.BlockSpec(memory_space=pl.ANY)
    wide = jax.ShapeDtypeStruct((ROWS_DEV, HEADS * HEAD_DIM), BF16)
    narrow = jax.ShapeDtypeStruct((ROWS_DEV, KV_HEADS * HEAD_DIM), BF16)
    all_rows = (2, TILES * PAIR, HEAD_DIM)
    results = pl.pallas_call(
        functools.partial(kernel, n_dp, n_blocks),
        out_shape=(wide, wide, narrow, narrow),
        in_specs=[hbm, vmem, vmem, hbm, vmem, smem, smem],
        out_specs=(hbm, hbm, vmem, vmem),
        scratch_shapes=[
            pltpu.VMEM((ROWS_DEV, HEADS * HEAD_DIM), BF16),
            pltpu.VMEM((ROWS_DEV, HEADS * HEAD_DIM), BF16),
            pltpu.VMEM((ROWS_DEV, HEADS * HEAD_DIM), BF16),
            pltpu.VMEM((ROWS_DEV, HEADS * HEAD_DIM), BF16),
            pltpu.VMEM((KV_HEADS, 4, 2, PAIR, 2 * HEAD_DIM), BF16),
            pltpu.VMEM((KV_HEADS, 2, 2 * HEAD_DIM, HALF), BF16),
            pltpu.VMEM((KV_HEADS, 2, 2 * HEAD_DIM, HALF), BF16),
            pltpu.VMEM((KV_HEADS, 2, 2 * HEAD_DIM, PAIR), BF16),
            pltpu.VMEM((KV_HEADS, 2, 2 * HEAD_DIM, PAIR), BF16),
            pltpu.VMEM((KV_HEADS, 2 * HEAD_DIM, HALF), BF16),
            pltpu.VMEM((KV_HEADS, 2 * HEAD_DIM, HALF), BF16),
            pltpu.VMEM((KV_HEADS, 4, 2 * HEAD_DIM, HALF), BF16),
            pltpu.VMEM((KV_HEADS, 4, 2 * HEAD_DIM, HALF), BF16),
            pltpu.VMEM((KV_HEADS, 4, 2 * HEAD_DIM, HALF), BF16),
            pltpu.VMEM((KV_HEADS, 4, 2 * HEAD_DIM, HALF), BF16),
            pltpu.VMEM((HEADS // 2, 2, HEAD_DIM, PAIR), BF16),
            pltpu.VMEM((HEADS // 2, 2, HEAD_DIM, PAIR), BF16),
            pltpu.VMEM((ROWS_DEV, HEADS * HEAD_DIM), BF16),
            pltpu.VMEM((3, HALF, PAIR), F32),
            pltpu.VMEM((2, VISITS, 2, HALF, PAIR), F32),
            pltpu.VMEM((VISITS, TILES, PAIR, PAIR), BF16),
            pltpu.VMEM((3, 4, 2, 2 * HEAD_DIM, PAIR), F32),
            pltpu.VMEM((2, 2, 2, HALF, HALF), F32),
            pltpu.VMEM((2, 2, HALF, PAIR), F32),
            pltpu.VMEM(all_rows, F32),
            pltpu.VMEM(all_rows, F32),
            pltpu.VMEM(all_rows, F32),
            pltpu.VMEM((2, TILES, HEAD_DIM, PAIR), BF16),
            pltpu.VMEM((2, TILES, HEAD_DIM, PAIR), BF16),
            pltpu.VMEM((SPAN_MAX, 8, 128), F32),
            pltpu.VMEM((n_dp, 8, 128), F32),
            pltpu.VMEM((n_blocks, 8, 128), F32),
            pltpu.VMEM((8, 128), F32),
            pltpu.SemaphoreType.DMA((2, KV_HEADS)),
            pltpu.SemaphoreType.DMA((2, KV_HEADS)),
            pltpu.SemaphoreType.DMA((KV_HEADS,)),
            pltpu.SemaphoreType.DMA((KV_HEADS,)),
            pltpu.SemaphoreType.DMA((KV_HEADS, 2, 2)),
            pltpu.SemaphoreType.DMA((KV_HEADS, 2, 2)),
            pltpu.SemaphoreType.DMA((KV_HEADS, 2)),
            pltpu.SemaphoreType.DMA((KV_HEADS, 2)),
            pltpu.SemaphoreType.DMA((KV_HEADS, 4)),
            pltpu.SemaphoreType.DMA((KV_HEADS, 4)),
            pltpu.SemaphoreType.DMA((KV_HEADS, 4)),
            pltpu.SemaphoreType.DMA((KV_HEADS, 4)),
            pltpu.SemaphoreType.DMA((KV_HEADS, 2)),
            pltpu.SemaphoreType.DMA((KV_HEADS, 2)),
            pltpu.SemaphoreType.DMA((KV_HEADS, 2)),
            pltpu.SemaphoreType.DMA((KV_HEADS, 2)),
            pltpu.SemaphoreType.DMA((KV_HEADS,)),
            pltpu.SemaphoreType.DMA((KV_HEADS,)),
            pltpu.SemaphoreType.DMA((KV_HEADS, 4)),
            pltpu.SemaphoreType.DMA((KV_HEADS, 4)),
            pltpu.SemaphoreType.DMA((KV_HEADS, 4)),
            pltpu.SemaphoreType.DMA((KV_HEADS, 4)),
            pltpu.SemaphoreType.DMA((24,)),
            pltpu.SemaphoreType.DMA((24,)),
        ],
        compiler_params=pltpu.CompilerParams(
            collective_id=0, has_side_effects=True, vmem_limit_bytes=56 * 1024 * 1024
        ),
    )(
        queries,
        key_states,
        value_states,
        grad_out,
        token_weight.reshape(1, ROWS_DEV),
        span_size,
        jnp.swapaxes(short_lengths, 1, 2),
    )
    return carry_out(*results)


def solution(mesh):
    rows = P(("dp", "cp"), None)
    n_dp = mesh.shape["dp"]
    n_blocks = mesh.shape["cp"] // SPAN_MAX
    return jax.shard_map(
        functools.partial(on_device, n_dp, n_blocks),
        mesh=mesh,
        in_specs=(rows, rows, rows, rows, P(("dp", "cp")), P("dp", None), P("dp", None, None)),
        out_specs=(rows, rows, rows, rows),
        check_vma=False,
    )
```
